32 devices in a mesh: shard: 2 (over x), rows: 16 (over z, y, core), dims: 1.
Axes of the slice: x: 2, y: 2, z: 4, core: 2. Of those that a mesh axis runs over, the one named last changes fastest.
Arguments:
- train_grads: bfloat16 [32768, 4096], P(('shard', 'rows'), 'dims'), parts along dimension 0, may hold values from -6 to 6
- query_grads: bfloat16 [4096, 4096], P(('shard', 'rows'), 'dims'), parts along dimension 0, may hold values from -6 to 6
- pair_query: int32 [256, 8], P(('shard', 'rows')), parts along dimension 0, may hold values from 0 to 15, all different within a row
- layer_slot: int32 [16], replicated, may hold values from 0 to 15, each once
- in_factor: float32 [16, 16, 16], replicated, may hold values from -1.5 to 1.5
- out_factor: float32 [16, 16, 16], replicated, may hold values from -1.5 to 1.5
Outputs:
- scores: float32 [256, 8, 128, 128], P(('shard', 'rows'), None, 'dims'), parts along dimension 0
The draws below stay inside these ranges and needn't reach their ends.
There are 2 independent parts, one for each index of `shard`. The reference program is written for one: setup_inputs(seed, part) draws one part's arguments, and reference() takes and returns one part's arrays. A program takes and returns all parts, laid end to end along the dimension named above; an argument that names none is the same for every part. Nothing has to cross between parts.
Inputs may be any that keep to these rules, and one draw needn't show every extreme that they name: `pair_query`: the 8 query blocks of one training block are distinct; every query block is named somewhere. `layer_slot`: each slot holds exactly one layer.
All inputs are finite; a program needn't handle non-finite values.
Results may differ from the reference program's by a relative error of at most 0.0029.
Values may be sent and summed in bfloat16 or wider, within the bound.
No kernel may reach another device: no remote copies, remote signals or barrier semaphores. Data moves between devices by JAX's collectives and lax.ppermute only.
A program may use at most 128 MiB of HBM per device.

```python
import jax
import jax.numpy as jnp
from jax import lax

PROJ = 16
LAYERS = 16
BLK = 128
SLOTS = 8
GDIM = 4096
QBLOCKS = 16
TBLOCKS = 128


def level_of(key, shape, shards, low, top_value):
    def one(axis_at, blocks):
        heights = jax.random.uniform(jax.random.fold_in(jax.random.fold_in(key, 6), axis_at), (blocks,), jnp.float32, low / len(shards), top_value / len(shards))
        return jnp.repeat(jnp.exp(heights), shape[axis_at] // blocks).reshape((-1,) + (1,) * (len(shape) - axis_at - 1))

    factor_of = one(*shards[0])
    for cut in shards[1:]:
        factor_of = factor_of * one(*cut)
    return factor_of


def choose_distinct(own_key, rows, amount, top, lift):
    order = jax.random.permutation(jax.random.fold_in(own_key, 1), amount)
    boost = order
    for power in range(3):
        boost = boost * boost // amount
    boost = boost * lift // amount
    lots = jax.random.randint(jax.random.fold_in(own_key, 2), (rows, amount), 0, 4096) + boost
    holders = jax.random.permutation(jax.random.fold_in(own_key, 3), rows)[jnp.arange(amount) % rows]
    lots = jnp.where(jnp.arange(rows)[:, None] == holders[None, :], 1 << 14, lots)
    priority = lots * amount + jnp.arange(amount)
    return lax.top_k(priority.astype(jnp.int32), top)[1].astype(jnp.int32)


def noise(rng, dims, spread, reach, shards=(), kind=jnp.bfloat16):
    gain = level_of(rng, dims, shards, -0.22, 0.18) if shards else 1.0
    drawn = jax.random.normal(rng, dims, jnp.float32) * spread * gain
    return jnp.minimum(jnp.maximum(drawn, -reach), reach).astype(kind)


def setup_inputs(seed: int = 0, part: int = 0) -> dict:
    splits = jax.random.split(jax.random.key(seed), 7)
    part_keys = jax.random.split(jax.random.fold_in(splits[6], part), 7)
    train_grads = noise(part_keys[0], (TBLOCKS * BLK, GDIM), 1.0, 6.0, ((0, 16),))
    query_grads = noise(part_keys[1], (QBLOCKS * BLK, GDIM), 1.0, 6.0, ((0, 16),))
    pair_query = choose_distinct(part_keys[2], TBLOCKS, QBLOCKS, SLOTS, 8192)
    layer_slot = jax.random.permutation(splits[3], LAYERS).astype(jnp.int32)
    in_factor = noise(splits[4], (LAYERS, PROJ, PROJ), PROJ ** -0.5, 1.5, (), jnp.float32)
    out_factor = noise(splits[5], (LAYERS, PROJ, PROJ), PROJ ** -0.5, 1.5, (), jnp.float32)
    return {"train_grads": train_grads, "query_grads": query_grads, "pair_query": pair_query, "layer_slot": layer_slot, "in_factor": in_factor, "out_factor": out_factor}


def slot_factors(layer_slot, in_factor, out_factor):
    slots = jnp.arange(LAYERS, dtype=jnp.int32)
    onehot = (slots[:, None] == layer_slot[None, :]).astype(jnp.float32)
    a_fac = jnp.einsum("sl,lij->sij", onehot, in_factor, precision=lax.Precision.HIGHEST)
    b_fac = jnp.einsum("sl,lij->sij", onehot, out_factor, precision=lax.Precision.HIGHEST)
    return a_fac, b_fac


def reference(train_grads, query_grads, pair_query, layer_slot, in_factor, out_factor):
    a_fac, b_fac = slot_factors(layer_slot, in_factor, out_factor)
    nrow = query_grads.shape[0]
    query = query_grads.astype(jnp.float32).reshape(nrow, LAYERS, PROJ, PROJ)
    left = jnp.einsum("sia,rsab->rsib", a_fac, query, precision=lax.Precision.HIGHEST)
    both = jnp.einsum("rsib,sbo->rsio", left, b_fac, precision=lax.Precision.HIGHEST)
    precond = both.reshape(nrow, GDIM).astype(jnp.bfloat16)
    qblocks = precond.reshape(QBLOCKS, BLK, GDIM)
    tblocks = train_grads.reshape(TBLOCKS, BLK, GDIM)

    def one_block(items):
        tblock, ids = items
        chosen = qblocks[ids].astype(jnp.float32)
        return jnp.einsum("rg,kqg->krq", tblock.astype(jnp.float32), chosen)

    return lax.map(one_block, (tblocks, pair_query))
```

```python
import functools

import jax
import jax.numpy as jnp
from jax import lax
from jax.experimental import pallas as pl
from jax.experimental.pallas import tpu as pltpu
from jax.sharding import PartitionSpec as P

PROJ = 16
BLK = 128
SLOT = PROJ * PROJ
F32 = jnp.float32
BF16 = jnp.bfloat16
NT = (((1,), (1,)), ((), ()))


def split3(x):
    one = x.astype(BF16)
    rest = x - one.astype(F32)
    two = rest.astype(BF16)
    three = (rest - two.astype(F32)).astype(BF16)
    return jnp.concatenate([one, two, three], axis=1)


def factor_kernel(layers, half, slot_ref, a_ref, b_ref, q_ref, high_ref, low_ref, ready_ref, xa, xb):
    row = lax.broadcasted_iota(jnp.int32, (3 * PROJ, SLOT), 0) % PROJ
    col = lax.broadcasted_iota(jnp.int32, (3 * PROJ, SLOT), 1)
    pick_i = jnp.where(col // PROJ == row, 1.0, 0.0).astype(BF16)
    pick_o = jnp.where(col % PROJ == row, 1.0, 0.0).astype(BF16)
    xa[...] = jnp.dot(split3(a_ref[...]), pick_i, preferred_element_type=F32)
    xb[...] = jnp.dot(split3(b_ref[...]), pick_o, preferred_element_type=F32)

    @pl.loop(0, layers)
    def _(layer):
        at = pl.multiple_of(layer * PROJ, PROJ)
        left = xa[pl.ds(at, PROJ), :]
        right = xb[pl.ds(at, PROJ), :]
        full = (left[:, None, :] * right[None, :, :]).reshape(SLOT, SLOT)
        high = full.astype(BF16)
        slot = slot_ref[layer]
        high_ref[slot] = high
        low_ref[slot] = (full - high.astype(F32)).astype(BF16)

    for s in range(layers // 2):
        x = q_ref[:, half + s * SLOT : half + (s + 1) * SLOT]
        y = jnp.dot(x, high_ref[layers // 2 + s], preferred_element_type=F32)
        y += jnp.dot(x, low_ref[layers // 2 + s], preferred_element_type=F32)
        ready_ref[:, s * SLOT : (s + 1) * SLOT] = y.astype(BF16)


def make_factors(layer_slot, in_factor, out_factor, query):
    layers = in_factor.shape[0]
    half = query.shape[1] // 2
    a_rows = jnp.swapaxes(in_factor, 1, 2).reshape(layers * PROJ, PROJ)
    b_rows = out_factor.reshape(layers * PROJ, PROJ)
    vmem = pl.BlockSpec(memory_space=pltpu.VMEM)
    return pl.pallas_call(
        functools.partial(factor_kernel, layers, half),
        out_shape=[
            jax.ShapeDtypeStruct((layers, SLOT, SLOT), BF16),
            jax.ShapeDtypeStruct((layers, SLOT, SLOT), BF16),
            jax.ShapeDtypeStruct((query.shape[0], half), BF16),
        ],
        in_specs=[pl.BlockSpec(memory_space=pltpu.SMEM)] + [vmem] * 3,
        out_specs=[vmem] * 3,
        scratch_shapes=[pltpu.VMEM((layers * PROJ, SLOT), F32)] * 2,
        compiler_params=pltpu.CompilerParams(vmem_limit_bytes=24 << 20),
        cost_estimate=pl.CostEstimate(flops=3 << 29, bytes_accessed=6 << 20, transcendentals=0),
        name="factors",
    )(layer_slot, a_rows, b_rows, query)


def score_kernel(jobs, n_raw, n_ready, has_acc, emit, aliased, half, *refs):
    refs = list(refs)
    table = refs.pop(0)
    train = refs.pop(0)
    raw = [refs.pop(0) for _ in range(n_raw)]
    high = refs.pop(0) if n_raw else None
    low = refs.pop(0) if n_raw else None
    ready = [refs.pop(0) for _ in range(n_ready)]
    acc = refs.pop(0) if has_acc else None
    if aliased:
        refs.pop(0)
    out = refs.pop(0)
    t_v, q_v, raw_v, high_v, low_v, acc_v, s_v, sems, out_sems = refs
    n = len(jobs)
    depth = t_v.shape[1]
    first = 0 if n_raw else half
    blocks = t_v.shape[0] // BLK
    half_slots = half // SLOT
    copies = []

    def begin(src, dst):
        copy = pltpu.make_async_copy(src, dst, sems.at[len(copies)])
        copy.start()
        copies.append(copy)
        return copy

    waits = []
    if n_raw:
        for j, ref in enumerate(raw):
            waits.append(begin(ref, raw_v.at[pl.ds(j * BLK, BLK)]))
        waits.append(begin(high.at[pl.ds(0, half_slots)], high_v))
        waits.append(begin(low.at[pl.ds(0, half_slots)], low_v))
    later = []
    for j, ref in enumerate(ready):
        later.append(begin(ref, q_v.at[pl.ds(j * BLK, BLK), pl.ds(depth - half, half)]))
    step = 2 * BLK
    loads = []
    for m in range(t_v.shape[0] // step):
        loads.append(begin(train.at[pl.ds(m * step, step), pl.ds(first, depth)], t_v.at[pl.ds(m * step, step)]))
    if has_acc:
        acc_load = begin(acc, acc_v)
    for copy in waits:
        copy.wait()
    if n_raw:
        for s in range(half_slots):
            cols = slice(s * SLOT, (s + 1) * SLOT)
            x = raw_v[:, cols]
            y = jnp.dot(x, high_v[s], preferred_element_type=F32)
            y += jnp.dot(x, low_v[s], preferred_element_type=F32)
            q_v[:, cols] = y.astype(BF16)
    for copy in later:
        copy.wait()
    if has_acc:
        acc_load.wait()

    def put(t, j):
        return pltpu.make_async_copy(s_v.at[t, j], out.at[t, jnp.maximum(table[t, jobs[j]], 0)], out_sems.at[t, j])

    for m in range(t_v.shape[0] // step):
        loads[m].wait()
        s = lax.dot_general(t_v[m * step : (m + 1) * step], q_v[...], NT, preferred_element_type=F32)
        for u in range(step // BLK):
            t = m * (step // BLK) + u
            for j in range(n):
                part = s[u * BLK : (u + 1) * BLK, j * BLK : (j + 1) * BLK]
                if has_acc:
                    part += acc_v[t, j]
                if not emit:
                    out[t, j] = part
                else:
                    s_v[t, j] = part

                    @pl.when(table[t, jobs[j]] >= 0)
                    def _(t=t, j=j):
                        put(t, j).start()

    if emit:
        for t in range(blocks):
            for j in range(n):

                @pl.when(table[t, jobs[j]] >= 0)
                def _(t=t, j=j):
                    put(t, j).wait()


def score(table, train, jobs, raw=(), ready=(), factors=None, acc=None, out=None, emit=True, name="score"):
    n = len(jobs)
    rows, width = train.shape
    half = width // 2
    blocks = rows // BLK
    depth = half * (bool(raw) + bool(ready))
    any_spec = pl.BlockSpec(memory_space=pl.ANY)
    args = [table, train, *raw]
    if raw:
        args += list(factors)
    args += list(ready)
    if acc is not None:
        args.append(acc)
    aliases = {}
    if out is not None:
        aliases = {len(args): 0}
        args.append(out)
    if emit:
        shape, out_spec = (blocks, table.shape[1] // 2, BLK, BLK), any_spec
    else:
        shape, out_spec = (blocks, n, BLK, BLK), pl.BlockSpec(memory_space=pltpu.VMEM)
    slots = half // SLOT if raw else 1
    flat = (slots, SLOT, SLOT) if raw else (1, 16, 128)
    small = (16, 128)
    scratch = [
        pltpu.VMEM((rows, depth), BF16),
        pltpu.VMEM((n * BLK, depth), BF16),
        pltpu.VMEM((n * BLK, half) if raw else small, BF16),
        pltpu.VMEM(flat, BF16),
        pltpu.VMEM(flat, BF16),
        pltpu.VMEM((blocks, n, BLK, BLK) if acc is not None else (1, 1, 8, 128), F32),
        pltpu.VMEM((blocks, n, BLK, BLK) if emit else (1, 1, 8, 128), F32),
        pltpu.SemaphoreType.DMA((len(raw) + len(ready) + 8 + rows // (2 * BLK),)),
        pltpu.SemaphoreType.DMA((blocks, n)),
    ]
    body = functools.partial(
        score_kernel, tuple(jobs), len(raw), len(ready), acc is not None, emit, out is not None, half
    )
    return pl.pallas_call(
        body,
        out_shape=jax.ShapeDtypeStruct(shape, F32),
        in_specs=[pl.BlockSpec(memory_space=pltpu.SMEM)] + [any_spec] * (len(args) - 1),
        out_specs=out_spec,
        scratch_shapes=scratch,
        input_output_aliases=aliases,
        compiler_params=pltpu.CompilerParams(vmem_limit_bytes=32 << 20),
        cost_estimate=pl.CostEstimate(
            flops=2 * rows * n * BLK * depth, bytes_accessed=2 * rows * depth, transcendentals=0
        ),
        name=name,
    )(*args)


def after(x, *deps):
    return lax.optimization_barrier((x, *deps))[0]


def local_rings(train_grads, query_grads, pair_query, layer_slot, in_factor, out_factor):
    count = lax.axis_size("rows")
    me = lax.axis_index("rows")
    core, col, layer = me % 2, me // 2 % 2, me // 4
    height = count // 4

    def index(z, y, c):
        return (z % height * 2 + y) * 2 + c

    def ring(move):
        return [(i, index(*move(i // 4, i // 2 % 2, i % 2))) for i in range(count)]

    down = ring(lambda z, y, c: (z - 1, y, c))
    up = ring(lambda z, y, c: (z + 1, y, c))
    across = ring(lambda z, y, c: (z, 1 - y, c))
    twin = ring(lambda z, y, c: (z, y, 1 - c))

    def send(x, perm):
        return lax.ppermute(x, "rows", perm)

    places = [(dz, dy) for dz in (0, 1, -1, 2) for dy in (0, 1)]
    ids = jnp.stack([index(layer + dz, (col + dy) % 2, (core + dc) % 2) for dz, dy in places for dc in (0, 1)])
    slots = jnp.arange(1, pair_query.shape[1] + 1, dtype=jnp.int32)
    named = pair_query[:, :, None] == ids[None, None, :]
    table = jnp.sum(jnp.where(named, slots[None, :, None], 0), axis=1) - 1
    job = {place: (2 * i, 2 * i + 1) for i, place in enumerate(places)}

    half = query_grads.shape[1] // 2
    raw = query_grads[:, :half]
    got = {"h0": raw}
    links = {
        "z": [("a0", "h0", down), ("b0", "h0", up), ("b1", "h1", up), ("f0", "a0", down), ("f1", "b1", up), ("a1", "h1", down), ("xa1", "y1", down)],
        "y": [("y0", "h0", across), ("y1", "h1", across), ("ya0", "a0", across), ("yb0", "b0", across), ("yb1", "b1", across), ("yf0", "f0", across), ("yf1", "f1", across)],
    }
    steps = len(links["z"])
    blocks = {
        (0, 0): ("h0", "h1"), (0, 1): ("y0", "y1"), (1, 0): ("a0", "a1"), (1, 1): ("ya0", "xa1"),
        (-1, 0): ("b0", "b1"), (-1, 1): ("yb0", "yb1"), (2, 0): ("f0", "f1"), (2, 1): ("yf0", "yf1"),
    }
    factors = None
    for s in range(steps):
        for way in ("z", "y"):
            name, source, perm = links[way][s]
            if source == "h1" and "h1" not in got:
                high, low, got["h1"] = make_factors(layer_slot, in_factor, out_factor, query_grads)
                factors = (high, low)
                for own in ("h0", "h1"):
                    got["c" + own] = send(got[own], twin)
            x = got[source]
            if s >= 2:
                past = [got[links[w][s - 2][0]] for w in ("z", "y")]
                x = after(x, *[v for v in past if v is not x])
            got[name] = send(x, perm)
            got["c" + name] = send(got[name], twin)

    def whole(place, out):
        first, second = blocks[place]
        return score(
            table, train_grads, job[place], raw=(got[first], got["c" + first]),
            ready=(got[second], got["c" + second]), factors=factors, out=out, name="score_pair",
        )

    out = None
    for place in ((0, 0), (0, 1), (-1, 0), (-1, 1), (2, 0), (1, 0)):
        out = whole(place, out)
    own = [job[(1, 1)][0], job[(2, 1)][0]]
    other = [job[(1, 1)][1], job[(2, 1)][1]]
    acc = [
        score(table, train_grads, jobs, raw=[got[p + n] for n in ("ya0", "yf0")], factors=factors, emit=False, name="score_first")
        for jobs, p in ((own, ""), (other, "c"))
    ]
    for jobs, p, part in ((own, "", acc[0]), (other, "c", acc[1])):
        out = score(table, train_grads, jobs, ready=[got[p + n] for n in ("xa1", "yf1")], acc=part, out=out, name="score_second")
    return out


def local(train_grads, query_grads, pair_query, layer_slot, in_factor, out_factor):
    dims_count = lax.axis_size("dims")
    dims_index = lax.axis_index("dims")
    width = query_grads.shape[1]
    local_layers = width // SLOT
    slots = dims_index * local_layers + jnp.arange(local_layers, dtype=jnp.int32)
    onehot = (slots[:, None] == layer_slot[None, :]).astype(F32)
    a_fac = jnp.einsum("sl,lij->sij", onehot, in_factor, precision=lax.Precision.HIGHEST)
    b_fac = jnp.einsum("sl,lij->sij", onehot, out_factor, precision=lax.Precision.HIGHEST)
    nrow = query_grads.shape[0]
    query = query_grads.astype(F32).reshape(nrow, local_layers, PROJ, PROJ)
    left = jnp.einsum("sia,rsab->rsib", a_fac, query, precision=lax.Precision.HIGHEST)
    both = jnp.einsum("rsib,sbo->rsio", left, b_fac, precision=lax.Precision.HIGHEST)
    precond = both.reshape(nrow, width).astype(BF16)
    gathered = lax.all_gather(precond, "rows", axis=0, tiled=True)
    qblocks = gathered.reshape(gathered.shape[0] // BLK, BLK, width)
    tblocks = train_grads.reshape(train_grads.shape[0] // BLK, BLK, width)

    def one_block(items):
        tblock, ids = items
        chosen = qblocks[ids]
        return jnp.einsum("rg,kqg->krq", tblock, chosen, preferred_element_type=F32)

    partial_scores = lax.map(one_block, (tblocks, pair_query))
    summed = lax.psum(partial_scores, "dims")
    share = BLK // dims_count
    return lax.dynamic_slice_in_dim(summed, dims_index * share, share, 2)


def solution(mesh):
    in_specs = (
        P(("shard", "rows"), "dims"),
        P(("shard", "rows"), "dims"),
        P(("shard", "rows"), None),
        P(),
        P(),
        P(),
    )
    out_specs = P(("shard", "rows"), None, "dims", None)
    four = mesh.shape["rows"] == 16 and mesh.shape["dims"] == 1
    body = local_rings if four else local
    return jax.shard_map(body, mesh=mesh, in_specs=in_specs, out_specs=out_specs, check_vma=False)
```

```python
import functools

import jax
import jax.numpy as jnp
from jax import lax
from jax.experimental import pallas as pl
from jax.experimental.pallas import tpu as pltpu
from jax.sharding import PartitionSpec as P

PROJ = 16
BLK = 128
SLOT = PROJ * PROJ
F32 = jnp.float32
BF16 = jnp.bfloat16
NT = (((1,), (1,)), ((), ()))
SMALL = pl.CostEstimate(flops=1, bytes_accessed=1, transcendentals=0)


def split3(x):
    one = x.astype(BF16)
    rest = x - one.astype(F32)
    two = rest.astype(BF16)
    three = (rest - two.astype(F32)).astype(BF16)
    return jnp.concatenate([one, two, three], axis=1)


def split3(x):
    one = x.astype(BF16)
    rest = x - one.astype(F32)
    two = rest.astype(BF16)
    three = (rest - two.astype(F32)).astype(BF16)
    return one, two, three


def precondition(x_refs, y_refs, high, low, skip):
    rows = x_refs[0].shape[0]
    for s in range(x_refs[0].shape[1] // SLOT):
        cols = slice(s * SLOT, (s + 1) * SLOT)
        x = jnp.concatenate([ref[:, cols] for ref in x_refs], axis=0)
        y = jnp.dot(x, high[skip + s], preferred_element_type=F32)
        y += jnp.dot(x, low[skip + s], preferred_element_type=F32)
        for i, ref in enumerate(y_refs):
            ref[:, cols] = y[i * rows : (i + 1) * rows].astype(BF16)


def prepare_kernel(
    layers, slot_ref, pair_ref, a_ref, b_ref, x0, x1, train, high_ref, low_ref, y0, y1, keep, away, table, xa, xb, sems
):
    me = lax.axis_index("rows")
    core = me & 1
    half = keep.shape[1]
    mine = pl.multiple_of(core * half, half)
    other = pl.multiple_of((1 - core) * half, half)
    loads = [
        pltpu.make_async_copy(train.at[:, pl.ds(other, half)], away, sems.at[0]),
        pltpu.make_async_copy(train.at[:, pl.ds(mine, half)], keep, sems.at[1]),
    ]
    for load in loads:
        load.start()
    row = lax.broadcasted_iota(jnp.int32, (PROJ, SLOT), 0)
    col = lax.broadcasted_iota(jnp.int32, (PROJ, SLOT), 1)
    pick_i = jnp.where(col // PROJ == row, 1.0, 0.0).astype(BF16)
    pick_o = jnp.where(col % PROJ == row, 1.0, 0.0).astype(BF16)
    total = 0.0
    for part in split3(b_ref[...]):
        total += jnp.dot(part, pick_o, preferred_element_type=F32)
    xb[...] = total
    for layer in range(layers):
        at = slice(layer * PROJ, (layer + 1) * PROJ)
        total = 0.0
        for part in split3(a_ref[at]):
            total += lax.dot_general(part, pick_i, (((0,), (0,)), ((), ())), preferred_element_type=F32)
        xa[at] = total

    @pl.loop(0, layers)
    def _(layer):
        slot = slot_ref[layer] - core * (layers // 2)

        @pl.when((slot >= 0) & (slot < layers // 2))
        def _():
            at = pl.multiple_of(layer * PROJ, PROJ)
            left = xa[pl.ds(at, PROJ), :]
            right = xb[pl.ds(at, PROJ), :]
            full = (left[:, None, :] * right[None, :, :]).reshape(SLOT, SLOT)
            high = full.astype(BF16)
            high_ref[slot] = high
            low_ref[slot] = (full - high.astype(F32)).astype(BF16)

    precondition([x0, x1], [y0, y1], high_ref, low_ref)
    blocks, slots = pair_ref.shape
    for t in range(blocks):
        for j in range(table.shape[1]):
            table[t, j] = -1
    for t in range(blocks):
        for k in range(slots):
            q = pair_ref[t, k]
            table[t, (((q >> 2) - (me >> 2)) & 3) * 4 + ((q ^ me) & 3)] = k
    for load in loads:
        load.wait()


def prepare(layer_slot, pair_query, in_factor, out_factor, x0, x1, train, jobs):
    layers = in_factor.shape[0]
    a_rows = in_factor.reshape(layers * PROJ, PROJ)
    b_rows = out_factor.reshape(layers * PROJ, PROJ)
    vmem = pl.BlockSpec(memory_space=pltpu.VMEM)
    smem = pl.BlockSpec(memory_space=pltpu.SMEM)
    side = jax.ShapeDtypeStruct((train.shape[0], train.shape[1] // 2), BF16)
    factor = jax.ShapeDtypeStruct((layers // 2, SLOT, SLOT), BF16)
    piece = jax.ShapeDtypeStruct(x0.shape, BF16)
    return pl.pallas_call(
        functools.partial(prepare_kernel, layers),
        out_shape=[factor, factor, piece, piece, side, side, jax.ShapeDtypeStruct((pair_query.shape[0], jobs), jnp.int32)],
        in_specs=[smem] * 2 + [vmem] * 4 + [pl.BlockSpec(memory_space=pl.ANY)],
        out_specs=[vmem] * 6 + [smem],
        scratch_shapes=[
            pltpu.VMEM((layers * PROJ, SLOT), F32),
            pltpu.VMEM((layers * PROJ, SLOT), F32),
            pltpu.SemaphoreType.DMA((2,)),
        ],
        compiler_params=pltpu.CompilerParams(vmem_limit_bytes=40 << 20),
        cost_estimate=SMALL,
        name="prepare",
    )(layer_slot, pair_query, a_rows, b_rows, x0, x1, train)


def precondition(x_refs, y_refs, high, low):
    rows = x_refs[0].shape[0]
    for s in range(x_refs[0].shape[1] // SLOT):
        cols = slice(s * SLOT, (s + 1) * SLOT)
        x = jnp.concatenate([ref[:, cols] for ref in x_refs], axis=0)
        y = jnp.dot(x, high[s], preferred_element_type=F32)
        y += jnp.dot(x, low[s], preferred_element_type=F32)
        for i, ref in enumerate(y_refs):
            ref[:, cols] = y[i * rows : (i + 1) * rows].astype(BF16)


def ready_kernel(x0, x1, high, low, y0, y1):
    precondition([x0, x1], [y0, y1], high, low)


def make_ready(x0, x1, high, low):
    return pl.pallas_call(
        ready_kernel,
        out_shape=[jax.ShapeDtypeStruct(x0.shape, BF16)] * 2,
        compiler_params=pltpu.CompilerParams(vmem_limit_bytes=10 << 20),
        cost_estimate=SMALL,
        name="ready",
    )(x0, x1, high, low)


def stage_kernel(adds, n_sums, n_train, n_pieces, aliased, *refs):
    refs = list(refs)
    table = refs.pop(0)
    sums = [refs.pop(0) for _ in range(n_sums)]
    trains = [refs.pop(0) for _ in range(n_train)]
    pieces = [refs.pop(0) for _ in range(n_pieces)]
    if aliased:
        refs.pop(0)
    token = refs.pop(0)
    out = refs.pop(0) if adds else None
    parts = [refs.pop(0) for _ in range(n_train)]
    token[...] = jnp.zeros_like(token)
    puts = []
    if adds:
        s_v, sems = refs
        for i, (job, ours, j, theirs, k) in enumerate(adds):
            for t in range(table.shape[0]):
                slot = table[t, job]
                copy = pltpu.make_async_copy(s_v.at[t, i], out.at[t, jnp.maximum(slot, 0)], sems.at[t, i])
                puts.append((slot >= 0, copy))
                s_v[t, i] = sums[ours][t, j] + sums[theirs][t, k]

                @pl.when(slot >= 0)
                def _(copy=copy):
                    copy.start()

    step = 2 * BLK
    for train, part in zip(trains, parts):
        for m in range(train.shape[0] // step):
            for h in range(0, n_pieces, 2):
                q = jnp.concatenate([ref[...] for ref in pieces[h : h + 2]], axis=0)
                s = lax.dot_general(train[m * step : (m + 1) * step], q, NT, preferred_element_type=F32)
                for u in range(step // BLK):
                    for j in range(2):
                        part[m * (step // BLK) + u, h + j] = s[u * BLK : (u + 1) * BLK, j * BLK : (j + 1) * BLK]

    for named, copy in puts:

        @pl.when(named)
        def _(copy=copy):
            copy.wait()


def stage(table, adds, trains, pieces, out, slots, cost=0):
    any_spec = pl.BlockSpec(memory_space=pl.ANY)
    vmem = pl.BlockSpec(memory_space=pltpu.VMEM)
    sums, spots = [], []
    for job, *pair in adds:
        spot = [job]
        for array, column in pair:
            at = next((i for i, other in enumerate(sums) if other is array), len(sums))
            if at == len(sums):
                sums.append(array)
            spot += [at, column]
        spots.append(tuple(spot))
    args = [table, *sums, *trains, *pieces]
    specs = [pl.BlockSpec(memory_space=pltpu.SMEM)] + [vmem] * (len(args) - 1)
    aliases = {}
    if adds and out is not None:
        aliases = {len(args): 1}
        args.append(out)
        specs.append(any_spec)
    blocks = table.shape[0]
    shapes, out_specs, scratch = [jax.ShapeDtypeStruct((8, 128), F32)], [vmem], []
    if adds:
        shapes.append(jax.ShapeDtypeStruct((blocks, slots, BLK, BLK), F32))
        out_specs.append(any_spec)
        scratch = [pltpu.VMEM((blocks, len(adds), BLK, BLK), F32), pltpu.SemaphoreType.DMA((blocks, len(adds)))]
    for _ in trains:
        shapes.append(jax.ShapeDtypeStruct((blocks, len(pieces), BLK, BLK), F32))
        out_specs.append(vmem)
    body = functools.partial(stage_kernel, tuple(spots), len(sums), len(trains), len(pieces), bool(aliases))
    token, *rest = pl.pallas_call(
        body,
        out_shape=shapes,
        in_specs=specs,
        out_specs=out_specs,
        scratch_shapes=scratch,
        input_output_aliases=aliases,
        compiler_params=pltpu.CompilerParams(vmem_limit_bytes=20 << 20),
        cost_estimate=pl.CostEstimate(flops=cost * 10**9, bytes_accessed=1, transcendentals=0),
        name="stage",
    )(*args)
    if adds:
        out = rest.pop(0)
    return token, out, rest


def after(x, *deps):
    return lax.optimization_barrier((x, *deps))[0]


def local_rings(train_grads, query_grads, pair_query, layer_slot, in_factor, out_factor):
    count = lax.axis_size("rows")
    height = count // 4

    def index(z, y, c):
        return (z % height * 2 + y) * 2 + c

    def ring(move):
        return [(i, index(*move(i // 4, i // 2 % 2, i % 2))) for i in range(count)]

    down = ring(lambda z, y, c: (z - 1, y, c))
    up = ring(lambda z, y, c: (z + 1, y, c))
    across = ring(lambda z, y, c: (z, 1 - y, c))
    twin = ring(lambda z, y, c: (z, y, 1 - c))

    def send(x, perm, name):
        with jax.named_scope("send_" + name):
            return lax.ppermute(x, "rows", perm)

    job = {}
    for letter, dz, dy in (("h", 0, 0), ("y", 0, 1), ("a", 1, 0), ("ya", 1, 1), ("f", 2, 0), ("yf", 2, 1), ("b", 3, 0), ("yb", 3, 1)):
        for dc in (0, 1):
            job[letter + str(dc)] = (dz * 2 + dy) * 2 + dc
    job["xa1"] = job.pop("ya1")
    other_name = {n: ("xa1" if n == "ya0" else "ya0" if n == "xa1" else n[:-1] + "10"[int(n[-1])]) for n in job}
    plan = [
        (("a0", "h0", down), ("y0", "h0", across)),
        (("b0", "h0", up), ("y1", "h1", across)),
        (("b1", "h1", up), ("ya0", "a0", across)),
        (("f0", "a0", down), ("yb0", "b0", across)),
        (("f1", "b1", up), ("yb1", "b1", across)),
        (("a1", "h1", down), ("yf0", "f0", across)),
        (("xa1", "y1", down), ("yf1", "f1", across)),
    ]
    work = {4: ["h0", "h1", "a0", "y0"], 5: ["b0", "y1", "b1", "ya0"], 6: ["f0", "yb0", "f1", "yb1"], 7: ["a1", "yf0"]}
    adding = {4: 6, 5: 7, 6: 8, 7: 8}
    cost = {4: 1, 5: 1, 6: 1, 7: 8}
    slots = pair_query.shape[1]
    half = query_grads.shape[1] // 2
    core = lax.axis_index("rows") % 2
    low_half, high_half = query_grads[:, :half], query_grads[:, half:]
    raw = {"h0": jnp.where(core == 0, low_half, high_half)}
    raw["h1"] = send(jnp.where(core == 0, high_half, low_half), twin, "h1")
    for step in plan[:2]:
        for name, source, perm in step:
            raw[name] = send(raw[source], perm, name)
    high, low, own0, own1, keep, away, table = prepare(
        layer_slot, pair_query, in_factor, out_factor, raw["h0"], raw["h1"], train_grads, 2 * 8
    )
    got = {"h0": own0, "h1": own1}
    trains = (keep, send(away, twin, "train"))
    ours, theirs, open_jobs = {}, {}, list(other_name)
    out, tokens = None, []

    def ready_adds():
        done = [n for n in open_jobs if n in ours and other_name[n] in theirs]
        for n in done:
            open_jobs.remove(n)
        return [(job[n], ours[n], theirs[other_name[n]]) for n in done]

    arriving = {}
    for s in range(2, len(plan) + 1):
        names = [name for name, _, _ in plan[s - 2]]
        if s < 4:
            got[names[0]], got[names[1]] = make_ready(raw[names[0]], raw[names[1]], high, low)
        past = [got[name] for name in names] + tokens
        if s < len(plan):
            for name, source, perm in plan[s]:
                deps = [v for v in past if v is not got[source]]
                got[name] = send(after(got[source], *deps), perm, name)
        if s not in work:
            continue
        for part in arriving.pop(s, []):
            theirs.update(part)
        pieces = [got[n] for n in work[s]]
        pieces[0] = after(pieces[0], *[got[name] for name in names if name not in work[s][:1]])
        token, out, (mine, away) = stage(table, ready_adds(), trains, pieces, out, slots, cost[s])
        tokens = [token]
        away = send(away, twin, "part" + str(s))
        ours.update({n: (mine, i) for i, n in enumerate(work[s])})
        arriving.setdefault(adding[s], []).append({n: (away, i) for i, n in enumerate(work[s])})
    names = [name for name, _, _ in plan[-1]]
    pieces = [after(got[names[0]], *tokens), got[names[1]]]
    _, _, (away,) = stage(table, [], trains[1:], pieces, out, slots)
    away = send(away, twin, "part")
    for part in arriving.pop(8, []):
        theirs.update(part)
    _, out, (mine,) = stage(table, ready_adds(), trains[:1], pieces, out, slots)
    ours.update({n: (mine, i) for i, n in enumerate(names)})
    theirs.update({n: (away, i) for i, n in enumerate(names)})
    _, out, _ = stage(table, ready_adds(), [], [], out, slots)
    return out


def local(train_grads, query_grads, pair_query, layer_slot, in_factor, out_factor):
    dims_count = lax.axis_size("dims")
    dims_index = lax.axis_index("dims")
    width = query_grads.shape[1]
    local_layers = width // SLOT
    slots = dims_index * local_layers + jnp.arange(local_layers, dtype=jnp.int32)
    onehot = (slots[:, None] == layer_slot[None, :]).astype(F32)
    a_fac = jnp.einsum("sl,lij->sij", onehot, in_factor, precision=lax.Precision.HIGHEST)
    b_fac = jnp.einsum("sl,lij->sij", onehot, out_factor, precision=lax.Precision.HIGHEST)
    nrow = query_grads.shape[0]
    query = query_grads.astype(F32).reshape(nrow, local_layers, PROJ, PROJ)
    left = jnp.einsum("sia,rsab->rsib", a_fac, query, precision=lax.Precision.HIGHEST)
    both = jnp.einsum("rsib,sbo->rsio", left, b_fac, precision=lax.Precision.HIGHEST)
    precond = both.reshape(nrow, width).astype(BF16)
    gathered = lax.all_gather(precond, "rows", axis=0, tiled=True)
    qblocks = gathered.reshape(gathered.shape[0] // BLK, BLK, width)
    tblocks = train_grads.reshape(train_grads.shape[0] // BLK, BLK, width)

    def one_block(items):
        tblock, ids = items
        chosen = qblocks[ids]
        return jnp.einsum("rg,kqg->krq", tblock, chosen, preferred_element_type=F32)

    partial_scores = lax.map(one_block, (tblocks, pair_query))
    summed = lax.psum(partial_scores, "dims")
    share = BLK // dims_count
    return lax.dynamic_slice_in_dim(summed, dims_index * share, share, 2)


def solution(mesh):
    in_specs = (
        P(("shard", "rows"), "dims"),
        P(("shard", "rows"), "dims"),
        P(("shard", "rows"), None),
        P(),
        P(),
        P(),
    )
    out_specs = P(("shard", "rows"), None, "dims", None)
    four = mesh.shape["rows"] == 16 and mesh.shape["dims"] == 1
    body = local_rings if four else local
    return jax.shard_map(body, mesh=mesh, in_specs=in_specs, out_specs=out_specs, check_vma=False)
```

```python
import functools

import jax
import jax.numpy as jnp
from jax import lax
from jax.experimental import pallas as pl
from jax.experimental.pallas import tpu as pltpu
from jax.sharding import PartitionSpec as P

PROJ = 16
BLK = 128
SLOT = PROJ * PROJ
F32 = jnp.float32
HALVES_LIMIT = 44
BF16 = jnp.bfloat16
NT = (((1,), (1,)), ((), ()))
SMALL = pl.CostEstimate(flops=10**9, bytes_accessed=1, transcendentals=0)


def split3(x):
    one = x.astype(BF16)
    rest = x - one.astype(F32)
    two = rest.astype(BF16)
    three = (rest - two.astype(F32)).astype(BF16)
    return jnp.concatenate([one, two, three], axis=1)


def split3(x):
    one = x.astype(BF16)
    rest = x - one.astype(F32)
    two = rest.astype(BF16)
    three = (rest - two.astype(F32)).astype(BF16)
    return one, two, three


def halves_kernel(train, twin_train, keep, rest, theirs, token, sems):
    token[...] = jnp.zeros_like(token)
    half = keep.shape[1]
    core = lax.axis_index("rows") & 1
    mine = pl.ds(pl.multiple_of(core * half, half), half)
    other = pl.ds(pl.multiple_of((1 - core) * half, half), half)
    copies = [
        pltpu.make_async_copy(train.at[:, mine], keep, sems.at[0]),
        pltpu.make_async_copy(twin_train.at[:, mine], theirs, sems.at[1]),
        pltpu.make_async_copy(train.at[:, other], rest, sems.at[2]),
    ]
    for copy in copies:
        copy.start()
    for copy in copies:
        copy.wait()


def make_halves(train, twin_train):
    side = jax.ShapeDtypeStruct((train.shape[0], train.shape[1] // 2), BF16)
    return pl.pallas_call(
        halves_kernel,
        out_shape=[side] * 3 + [jax.ShapeDtypeStruct((8, 128), F32)],
        in_specs=[pl.BlockSpec(memory_space=pl.ANY)] * 2,
        out_specs=[pl.BlockSpec(memory_space=pltpu.VMEM)] * 4,
        scratch_shapes=[pltpu.SemaphoreType.DMA((3,))],
        compiler_params=pltpu.CompilerParams(vmem_limit_bytes=HALVES_LIMIT << 20),
        cost_estimate=SMALL,
        name="halves",
    )(train, twin_train)


def precondition(x_refs, y_refs, high, low, skip):
    rows = x_refs[0].shape[0]
    for s in range(x_refs[0].shape[1] // SLOT):
        cols = slice(s * SLOT, (s + 1) * SLOT)
        x = jnp.concatenate([ref[:, cols] for ref in x_refs], axis=0)
        y = jnp.dot(x, high[skip + s], preferred_element_type=F32)
        y += jnp.dot(x, low[skip + s], preferred_element_type=F32)
        for i, ref in enumerate(y_refs):
            ref[:, cols] = y[i * rows : (i + 1) * rows].astype(BF16)


def prepare_kernel(layers, slot_ref, pair_ref, a_ref, b_ref, x0, x1, high_ref, low_ref, y0, y1, table, xa, xb):
    me = lax.axis_index("rows")
    core = me & 1
    row = lax.broadcasted_iota(jnp.int32, (PROJ, SLOT), 0)
    col = lax.broadcasted_iota(jnp.int32, (PROJ, SLOT), 1)
    pick_i = jnp.where(col // PROJ == row, 1.0, 0.0).astype(BF16)
    pick_o = jnp.where(col % PROJ == row, 1.0, 0.0).astype(BF16)
    total = 0.0
    for part in split3(b_ref[...]):
        total += jnp.dot(part, pick_o, preferred_element_type=F32)
    xb[...] = total
    for layer in range(layers):
        at = slice(layer * PROJ, (layer + 1) * PROJ)
        total = 0.0
        for part in split3(a_ref[at]):
            total += lax.dot_general(part, pick_i, (((0,), (0,)), ((), ())), preferred_element_type=F32)
        xa[at] = total

    @pl.loop(0, layers)
    def _(layer):
        slot = slot_ref[layer] - core * (layers // 2)

        @pl.when((slot >= 0) & (slot < layers // 2))
        def _():
            at = pl.multiple_of(layer * PROJ, PROJ)
            left = xa[pl.ds(at, PROJ), :]
            right = xb[pl.ds(at, PROJ), :]
            full = (left[:, None, :] * right[None, :, :]).reshape(SLOT, SLOT)
            high = full.astype(BF16)
            high_ref[slot] = high
            low_ref[slot] = (full - high.astype(F32)).astype(BF16)

    precondition([x0, x1], [y0, y1], high_ref, low_ref)
    blocks, slots = pair_ref.shape
    for t in range(blocks):
        for j in range(table.shape[1]):
            table[t, j] = -1
    for t in range(blocks):
        for k in range(slots):
            q = pair_ref[t, k]
            table[t, (((q >> 2) - (me >> 2)) & 3) * 4 + ((q ^ me) & 3)] = k


def prepare(layer_slot, pair_query, in_factor, out_factor, x0, x1, jobs):
    layers = in_factor.shape[0]
    a_rows = in_factor.reshape(layers * PROJ, PROJ)
    b_rows = out_factor.reshape(layers * PROJ, PROJ)
    vmem = pl.BlockSpec(memory_space=pltpu.VMEM)
    smem = pl.BlockSpec(memory_space=pltpu.SMEM)
    factor = jax.ShapeDtypeStruct((layers // 2, SLOT, SLOT), BF16)
    piece = jax.ShapeDtypeStruct(x0.shape, BF16)
    return pl.pallas_call(
        functools.partial(prepare_kernel, layers),
        out_shape=[factor, factor, piece, piece, jax.ShapeDtypeStruct((pair_query.shape[0], jobs), jnp.int32)],
        in_specs=[smem] * 2 + [vmem] * 4,
        out_specs=[vmem] * 4 + [smem],
        scratch_shapes=[
            pltpu.VMEM((layers * PROJ, SLOT), F32),
            pltpu.VMEM((layers * PROJ, SLOT), F32),
        ],
        compiler_params=pltpu.CompilerParams(vmem_limit_bytes=16 << 20),
        cost_estimate=SMALL,
        name="prepare",
    )(layer_slot, pair_query, a_rows, b_rows, x0, x1)


def halves_kernel(train, twin_train, keep, rest, theirs, token, sems):
    token[...] = jnp.zeros_like(token)
    half = keep.shape[1]
    core = lax.axis_index("rows") & 1
    mine = pl.ds(pl.multiple_of(core * half, half), half)
    other = pl.ds(pl.multiple_of((1 - core) * half, half), half)
    copies = [
        pltpu.make_async_copy(train.at[:, mine], keep, sems.at[0]),
        pltpu.make_async_copy(twin_train.at[:, mine], theirs, sems.at[1]),
        pltpu.make_async_copy(train.at[:, other], rest, sems.at[2]),
    ]
    for copy in copies:
        copy.start()
    for copy in copies:
        copy.wait()


def make_halves(train, twin_train):
    side = jax.ShapeDtypeStruct((train.shape[0], train.shape[1] // 2), BF16)
    return pl.pallas_call(
        halves_kernel,
        out_shape=[side] * 3 + [jax.ShapeDtypeStruct((8, 128), F32)],
        in_specs=[pl.BlockSpec(memory_space=pl.ANY)] * 2,
        out_specs=[pl.BlockSpec(memory_space=pltpu.VMEM)] * 4,
        scratch_shapes=[pltpu.SemaphoreType.DMA((3,))],
        compiler_params=pltpu.CompilerParams(vmem_limit_bytes=HALVES_LIMIT << 20),
        cost_estimate=SMALL,
        name="halves",
    )(train, twin_train)


def precondition(x_refs, y_refs, high, low):
    rows = x_refs[0].shape[0]
    for s in range(x_refs[0].shape[1] // SLOT):
        cols = slice(s * SLOT, (s + 1) * SLOT)
        x = jnp.concatenate([ref[:, cols] for ref in x_refs], axis=0)
        y = jnp.dot(x, high[s], preferred_element_type=F32)
        y += jnp.dot(x, low[s], preferred_element_type=F32)
        for i, ref in enumerate(y_refs):
            ref[:, cols] = y[i * rows : (i + 1) * rows].astype(BF16)


def ready_kernel(x0, x1, high, low, y0, y1):
    precondition([x0, x1], [y0, y1], high, low)


def make_ready(x0, x1, high, low):
    return pl.pallas_call(
        ready_kernel,
        out_shape=[jax.ShapeDtypeStruct(x0.shape, BF16)] * 2,
        compiler_params=pltpu.CompilerParams(vmem_limit_bytes=10 << 20),
        cost_estimate=SMALL,
        name="ready",
    )(x0, x1, high, low)


def stage_kernel(adds, products, n_arrays, n_idle, *refs):
    table, arrays, refs = refs[0], refs[1 : 1 + n_arrays], list(refs[1 + n_arrays + n_idle :])
    token = refs.pop(0)
    puts = len(adds) + sum(len(product[2]) for product in products)
    out = refs.pop(0) if puts else None
    parts = [None if product[2] else refs.pop(0) for product in products]
    token[...] = jnp.zeros_like(token)
    started = []

    def put(t, job, value):
        s_v, sems = refs
        at = len(started)
        i, j = at // table.shape[0], at % table.shape[0]
        slot = table[t, job]
        copy = pltpu.make_async_copy(s_v.at[i, j], out.at[t, jnp.maximum(slot, 0)], sems.at[i, j])
        s_v[i, j] = value
        started.append((slot >= 0, copy))

        @pl.when(slot >= 0)
        def _():
            copy.start()

    for job, ours, j, theirs, k in adds:
        for t in range(table.shape[0]):
            put(t, job, arrays[ours][t, j] + arrays[theirs][t, k])

    step = 2 * BLK
    for (train, pieces, sums, before), part in zip(products, parts):
        skip = 0
        if before is not None:
            skip = arrays[before].shape[1]
            part[:, :skip] = arrays[before][...]
        train = arrays[train]
        for m in range(train.shape[0] // step):
            for h in range(0, len(pieces), 2):
                q = jnp.concatenate([arrays[i][...] for i in pieces[h : h + 2]], axis=0)
                s = lax.dot_general(train[m * step : (m + 1) * step], q, NT, preferred_element_type=F32)
                for u in range(step // BLK):
                    for j in range(2):
                        t = m * (step // BLK) + u
                        value = s[u * BLK : (u + 1) * BLK, j * BLK : (j + 1) * BLK]
                        if sums:
                            job, at, column = sums[h + j]
                            put(t, job, value + arrays[at][t, column])
                        else:
                            part[t, skip + h + j] = value

    for named, copy in started:

        @pl.when(named)
        def _(copy=copy):
            copy.wait()


def stage(table, adds, products, out, slots, cost=0, wait=()):
    vmem = pl.BlockSpec(memory_space=pltpu.VMEM)
    arrays = []

    def index(array):
        for i, other in enumerate(arrays):
            if other is array:
                return i
        arrays.append(array)
        return len(arrays) - 1

    blocks = table.shape[0]
    adds = tuple((job, index(a), i, index(b), j) for job, (a, i), (b, j) in adds)
    shapes, out_specs, scratch = [jax.ShapeDtypeStruct((8, 128), F32)], [vmem], []
    puts = len(adds) + sum(len(product[2]) for product in products)
    if puts:
        shapes.append(jax.ShapeDtypeStruct((blocks, slots, BLK, BLK), F32))
        out_specs.append(pl.BlockSpec(memory_space=pl.ANY))
        scratch = [pltpu.VMEM((puts, blocks, BLK, BLK), F32), pltpu.SemaphoreType.DMA((puts, blocks))]
    spots = []
    for train, pieces, sums, before in products:
        if not sums:
            width = len(pieces) + (0 if before is None else before.shape[1])
            shapes.append(jax.ShapeDtypeStruct((blocks, width, BLK, BLK), F32))
            out_specs.append(vmem)
        spots.append((
            index(train), tuple(index(piece) for piece in pieces),
            tuple((job, index(array), i) for job, (array, i) in sums), None if before is None else index(before),
        ))
    args = [table, *arrays]
    specs = [pl.BlockSpec(memory_space=pltpu.SMEM)] + [vmem] * len(arrays)
    args += wait
    specs += [pl.BlockSpec(memory_space=pl.ANY)] * len(wait)
    aliased = bool(puts) and out is not None
    if aliased:
        args.append(out)
        specs.append(pl.BlockSpec(memory_space=pl.ANY))
    body = functools.partial(stage_kernel, adds, tuple(spots), len(arrays), len(wait) + aliased)
    token, *rest = pl.pallas_call(
        body,
        out_shape=shapes,
        in_specs=specs,
        out_specs=out_specs,
        scratch_shapes=scratch,
        input_output_aliases={len(args) - 1: 1} if aliased else {},
        compiler_params=pltpu.CompilerParams(vmem_limit_bytes=20 << 20),
        cost_estimate=pl.CostEstimate(flops=int(cost * 1.15e9), bytes_accessed=1, transcendentals=0),
        name="stage",
    )(*args)
    if puts:
        out = rest.pop(0)
    return token, out, rest


def pass_kernel(x_ref, y_ref):
    y_ref[...] = x_ref[...]


def stand(token, cost):
    return pl.pallas_call(
        pass_kernel,
        out_shape=jax.ShapeDtypeStruct(token.shape, token.dtype),
        compiler_params=pltpu.CompilerParams(vmem_limit_bytes=1 << 20),
        cost_estimate=pl.CostEstimate(flops=int(cost * 1.15e9), bytes_accessed=1, transcendentals=0),
        name="stand",
    )(token)


def after(x, *deps):
    return lax.optimization_barrier((x, *deps))[0]


def local_rings(train_grads, query_grads, pair_query, layer_slot, in_factor, out_factor):
    count = lax.axis_size("rows")
    height = count // 4

    def index(z, y, c):
        return (z % height * 2 + y) * 2 + c

    def ring(move):
        return [(i, index(*move(i // 4, i // 2 % 2, i % 2))) for i in range(count)]

    down = ring(lambda z, y, c: (z - 1, y, c))
    up = ring(lambda z, y, c: (z + 1, y, c))
    across = ring(lambda z, y, c: (z, 1 - y, c))
    twin = ring(lambda z, y, c: (z, y, 1 - c))

    def send(x, perm, name):
        with jax.named_scope("send_" + name):
            return lax.ppermute(x, "rows", perm)

    job = {}
    for letter, dz, dy in (("h", 0, 0), ("y", 0, 1), ("a", 1, 0), ("ya", 1, 1), ("f", 2, 0), ("yf", 2, 1), ("b", 3, 0), ("yb", 3, 1)):
        for dc in (0, 1):
            job[letter + str(dc)] = (dz * 2 + dy) * 2 + dc
    job["xa1"] = job.pop("ya1")
    other_name = {n: ("xa1" if n == "ya0" else "ya0" if n == "xa1" else n[:-1] + "10"[int(n[-1])]) for n in job}
    plan = [
        (("a0", "h0", down), ("y0", "h0", across)),
        (("b0", "h0", up), ("y1", "h1", across)),
        (("b1", "h1", up), ("ya0", "a0", across)),
        (("f0", "a0", down), ("yb0", "b0", across)),
        (("f1", "b1", up), ("yb1", "b1", across)),
        (("a1", "h1", down), ("yf0", "f0", across)),
        (("xa1", "y1", down), ("yf1", "f1", across)),
    ]
    work = {3: ["h0", "h1", "a0", "y0"], 4: ["b0", "y1", "b1", "ya0"], 5: ["f0", "yb0"], 6: ["f1", "yb1"], 7: ["a1", "yf0"]}
    exchange = (4, 6, 7)
    cost = {3: 1, 4: 1, 5: 1, 6: 1, 7: 1, 8: 12, 9: 1}
    stand_cost = 60
    slots = pair_query.shape[1]
    half = query_grads.shape[1] // 2
    core = lax.axis_index("rows") % 2
    low_half, high_half = query_grads[:, :half], query_grads[:, half:]
    raw = {"h0": jnp.where(core == 0, low_half, high_half)}
    raw["h1"] = send(jnp.where(core == 0, high_half, low_half), twin, "h1")
    for step in plan[:2]:
        for name, source, perm in step:
            raw[name] = send(raw[source], perm, name)
    high, low, own0, own1, table = prepare(
        layer_slot, pair_query, in_factor, out_factor, raw["h0"], raw["h1"], 2 * 8
    )
    got = {"h0": own0, "h1": own1}
    keep, rest, their_train, halves_token = make_halves(train_grads, send(train_grads, twin, "train"))
    ours, theirs, open_jobs = {}, {}, list(other_name)
    out, tokens = None, []

    def ready_adds():
        done = [n for n in open_jobs if n in ours and other_name[n] in theirs]
        for n in done:
            open_jobs.remove(n)
        return [(job[n], ours[n], theirs[other_name[n]]) for n in done]

    held, columns = None, []
    for s in range(2, len(plan) + 1):
        names = [name for name, _, _ in plan[s - 2]]
        if s < 4:
            got[names[0]], got[names[1]] = make_ready(raw[names[0]], raw[names[1]], high, low)
        past = [got[name] for name in names] + (tokens if s > 3 else [halves_token] * (s == 2))
        if s < len(plan):
            for name, source, perm in plan[s]:
                deps = [v for v in past if v is not got[source]]
                got[name] = send(after(got[source], *deps), perm, name)
        if s not in work:
            continue
        pieces = [got[n] for n in work[s]]
        products = [(keep, pieces, (), None), (their_train, pieces, (), held)]
        token, _, (mine, held) = stage(table, [], products, None, slots, cost[s], tokens)
        tokens = [token]
        ours.update({n: (mine, i) for i, n in enumerate(work[s])})
        columns += work[s]
        if s in exchange:
            part = send(held, twin, "part" + str(s))
            theirs.update({n: (part, i) for i, n in enumerate(columns)})
            held, columns = None, []
    late = {n: theirs.pop(n) for n in work[len(plan)]}
    adds = ready_adds()
    token, out, _ = stage(table, adds, [], None, slots, 1, [stand(tokens[0], stand_cost)])
    theirs.update(late)
    names = [name for name, _, _ in plan[-1]]
    pieces = [got[name] for name in names]
    twins = [send(after(piece, token), twin, "c" + name) for piece, name in zip(pieces, names)]
    _, _, (mine,) = stage(table, [], [(keep, pieces, (), None)], None, slots, cost[8], [token])
    ours.update({n: (mine, i) for i, n in enumerate(names)})
    adds = ready_adds()
    sums = tuple((job[other_name[name]], ours[other_name[name]]) for name in names)
    _, out, _ = stage(table, adds, [(rest, twins, sums, None)], out, slots, cost[9])
    return out


def local(train_grads, query_grads, pair_query, layer_slot, in_factor, out_factor):
    dims_count = lax.axis_size("dims")
    dims_index = lax.axis_index("dims")
    width = query_grads.shape[1]
    local_layers = width // SLOT
    slots = dims_index * local_layers + jnp.arange(local_layers, dtype=jnp.int32)
    onehot = (slots[:, None] == layer_slot[None, :]).astype(F32)
    a_fac = jnp.einsum("sl,lij->sij", onehot, in_factor, precision=lax.Precision.HIGHEST)
    b_fac = jnp.einsum("sl,lij->sij", onehot, out_factor, precision=lax.Precision.HIGHEST)
    nrow = query_grads.shape[0]
    query = query_grads.astype(F32).reshape(nrow, local_layers, PROJ, PROJ)
    left = jnp.einsum("sia,rsab->rsib", a_fac, query, precision=lax.Precision.HIGHEST)
    both = jnp.einsum("rsib,sbo->rsio", left, b_fac, precision=lax.Precision.HIGHEST)
    precond = both.reshape(nrow, width).astype(BF16)
    gathered = lax.all_gather(precond, "rows", axis=0, tiled=True)
    qblocks = gathered.reshape(gathered.shape[0] // BLK, BLK, width)
    tblocks = train_grads.reshape(train_grads.shape[0] // BLK, BLK, width)

    def one_block(items):
        tblock, ids = items
        chosen = qblocks[ids]
        return jnp.einsum("rg,kqg->krq", tblock, chosen, preferred_element_type=F32)

    partial_scores = lax.map(one_block, (tblocks, pair_query))
    summed = lax.psum(partial_scores, "dims")
    share = BLK // dims_count
    return lax.dynamic_slice_in_dim(summed, dims_index * share, share, 2)


def solution(mesh):
    in_specs = (
        P(("shard", "rows"), "dims"),
        P(("shard", "rows"), "dims"),
        P(("shard", "rows"), None),
        P(),
        P(),
        P(),
    )
    out_specs = P(("shard", "rows"), None, "dims", None)
    four = mesh.shape["rows"] == 16 and mesh.shape["dims"] == 1
    body = local_rings if four else local
    return jax.shard_map(body, mesh=mesh, in_specs=in_specs, out_specs=out_specs, check_vma=False)
```

```python
import functools

import jax
import jax.numpy as jnp
from jax import lax
from jax.experimental import pallas as pl
from jax.experimental.pallas import tpu as pltpu
from jax.sharding import PartitionSpec as P

PROJ = 16
BLK = 128
SLOT = PROJ * PROJ
F32 = jnp.float32
HALVES_LIMIT = 44
BF16 = jnp.bfloat16
NT = (((1,), (1,)), ((), ()))
SMALL = pl.CostEstimate(flops=10**9, bytes_accessed=1, transcendentals=0)


def split3(x):
    one = x.astype(BF16)
    rest = x - one.astype(F32)
    two = rest.astype(BF16)
    three = (rest - two.astype(F32)).astype(BF16)
    return jnp.concatenate([one, two, three], axis=1)


def split3(x):
    one = x.astype(BF16)
    rest = x - one.astype(F32)
    two = rest.astype(BF16)
    three = (rest - two.astype(F32)).astype(BF16)
    return one, two, three


def halves_kernel(train, twin_train, keep, rest, theirs, token, sems):
    token[...] = jnp.zeros_like(token)
    half = keep.shape[1]
    core = lax.axis_index("rows") & 1
    mine = pl.ds(pl.multiple_of(core * half, half), half)
    other = pl.ds(pl.multiple_of((1 - core) * half, half), half)
    copies = [
        pltpu.make_async_copy(train.at[:, mine], keep, sems.at[0]),
        pltpu.make_async_copy(twin_train.at[:, mine], theirs, sems.at[1]),
        pltpu.make_async_copy(train.at[:, other], rest, sems.at[2]),
    ]
    for copy in copies:
        copy.start()
    for copy in copies:
        copy.wait()


def make_halves(train, twin_train):
    side = jax.ShapeDtypeStruct((train.shape[0], train.shape[1] // 2), BF16)
    return pl.pallas_call(
        halves_kernel,
        out_shape=[side] * 3 + [jax.ShapeDtypeStruct((8, 128), F32)],
        in_specs=[pl.BlockSpec(memory_space=pl.ANY)] * 2,
        out_specs=[pl.BlockSpec(memory_space=pltpu.VMEM)] * 4,
        scratch_shapes=[pltpu.SemaphoreType.DMA((3,))],
        compiler_params=pltpu.CompilerParams(vmem_limit_bytes=HALVES_LIMIT << 20),
        cost_estimate=SMALL,
        name="halves",
    )(train, twin_train)


def precondition(x_refs, y_refs, high, low, skip):
    rows = x_refs[0].shape[0]
    for s in range(x_refs[0].shape[1] // SLOT):
        cols = slice(s * SLOT, (s + 1) * SLOT)
        x = jnp.concatenate([ref[:, cols] for ref in x_refs], axis=0)
        y = jnp.dot(x, high[skip + s], preferred_element_type=F32)
        y += jnp.dot(x, low[skip + s], preferred_element_type=F32)
        for i, ref in enumerate(y_refs):
            ref[:, cols] = y[i * rows : (i + 1) * rows].astype(BF16)


def prepare_kernel(layers, slot_ref, pair_ref, a_ref, b_ref, x0, x1, high_ref, low_ref, y0, y1, table, xa, xb):
    me = lax.axis_index("rows")
    core = me & 1
    row = lax.broadcasted_iota(jnp.int32, (PROJ, SLOT), 0)
    col = lax.broadcasted_iota(jnp.int32, (PROJ, SLOT), 1)
    pick_i = jnp.where(col // PROJ == row, 1.0, 0.0).astype(BF16)
    pick_o = jnp.where(col % PROJ == row, 1.0, 0.0).astype(BF16)
    total = 0.0
    for part in split3(b_ref[...]):
        total += jnp.dot(part, pick_o, preferred_element_type=F32)
    xb[...] = total
    for layer in range(layers):
        at = slice(layer * PROJ, (layer + 1) * PROJ)
        total = 0.0
        for part in split3(a_ref[at]):
            total += lax.dot_general(part, pick_i, (((0,), (0,)), ((), ())), preferred_element_type=F32)
        xa[at] = total

    @pl.loop(0, layers)
    def _(layer):
        slot = slot_ref[layer] - core * (layers // 2)

        @pl.when((slot >= 0) & (slot < layers // 2))
        def _():
            at = pl.multiple_of(layer * PROJ, PROJ)
            left = xa[pl.ds(at, PROJ), :]
            right = xb[pl.ds(at, PROJ), :]
            full = (left[:, None, :] * right[None, :, :]).reshape(SLOT, SLOT)
            high = full.astype(BF16)
            high_ref[slot] = high
            low_ref[slot] = (full - high.astype(F32)).astype(BF16)

    precondition([x0, x1], [y0, y1], high_ref, low_ref)
    blocks, slots = pair_ref.shape
    for t in range(blocks):
        for j in range(table.shape[1]):
            table[t, j] = -1
    for t in range(blocks):
        for k in range(slots):
            q = pair_ref[t, k]
            table[t, (((q >> 2) - (me >> 2)) & 3) * 4 + ((q ^ me) & 3)] = k


def prepare(layer_slot, pair_query, in_factor, out_factor, x0, x1, jobs):
    layers = in_factor.shape[0]
    a_rows = in_factor.reshape(layers * PROJ, PROJ)
    b_rows = out_factor.reshape(layers * PROJ, PROJ)
    vmem = pl.BlockSpec(memory_space=pltpu.VMEM)
    smem = pl.BlockSpec(memory_space=pltpu.SMEM)
    factor = jax.ShapeDtypeStruct((layers // 2, SLOT, SLOT), BF16)
    piece = jax.ShapeDtypeStruct(x0.shape, BF16)
    return pl.pallas_call(
        functools.partial(prepare_kernel, layers),
        out_shape=[factor, factor, piece, piece, jax.ShapeDtypeStruct((pair_query.shape[0], jobs), jnp.int32)],
        in_specs=[smem] * 2 + [vmem] * 4,
        out_specs=[vmem] * 4 + [smem],
        scratch_shapes=[
            pltpu.VMEM((layers * PROJ, SLOT), F32),
            pltpu.VMEM((layers * PROJ, SLOT), F32),
        ],
        compiler_params=pltpu.CompilerParams(vmem_limit_bytes=16 << 20),
        cost_estimate=SMALL,
        name="prepare",
    )(layer_slot, pair_query, a_rows, b_rows, x0, x1)


def halves_kernel(train, twin_train, keep, rest, theirs, token, sems):
    token[...] = jnp.zeros_like(token)
    half = keep.shape[1]
    core = lax.axis_index("rows") & 1
    mine = pl.ds(pl.multiple_of(core * half, half), half)
    other = pl.ds(pl.multiple_of((1 - core) * half, half), half)
    copies = [
        pltpu.make_async_copy(train.at[:, mine], keep, sems.at[0]),
        pltpu.make_async_copy(twin_train.at[:, mine], theirs, sems.at[1]),
        pltpu.make_async_copy(train.at[:, other], rest, sems.at[2]),
    ]
    for copy in copies:
        copy.start()
    for copy in copies:
        copy.wait()


def make_halves(train, twin_train):
    side = jax.ShapeDtypeStruct((train.shape[0], train.shape[1] // 2), BF16)
    return pl.pallas_call(
        halves_kernel,
        out_shape=[side] * 3 + [jax.ShapeDtypeStruct((8, 128), F32)],
        in_specs=[pl.BlockSpec(memory_space=pl.ANY)] * 2,
        out_specs=[pl.BlockSpec(memory_space=pltpu.VMEM)] * 4,
        scratch_shapes=[pltpu.SemaphoreType.DMA((3,))],
        compiler_params=pltpu.CompilerParams(vmem_limit_bytes=HALVES_LIMIT << 20),
        cost_estimate=SMALL,
        name="halves",
    )(train, twin_train)


def precondition(x_refs, y_refs, high, low):
    rows = x_refs[0].shape[0]
    for s in range(x_refs[0].shape[1] // SLOT):
        cols = slice(s * SLOT, (s + 1) * SLOT)
        x = jnp.concatenate([ref[:, cols] for ref in x_refs], axis=0)
        y = jnp.dot(x, high[s], preferred_element_type=F32)
        y += jnp.dot(x, low[s], preferred_element_type=F32)
        for i, ref in enumerate(y_refs):
            ref[:, cols] = y[i * rows : (i + 1) * rows].astype(BF16)


def ready_kernel(x0, x1, high, low, y0, y1):
    precondition([x0, x1], [y0, y1], high, low)


def make_ready(x0, x1, high, low):
    return pl.pallas_call(
        ready_kernel,
        out_shape=[jax.ShapeDtypeStruct(x0.shape, BF16)] * 2,
        compiler_params=pltpu.CompilerParams(vmem_limit_bytes=10 << 20),
        cost_estimate=SMALL,
        name="ready",
    )(x0, x1, high, low)


def stage_kernel(adds, products, n_arrays, n_idle, *refs):
    table, arrays, refs = refs[0], refs[1 : 1 + n_arrays], list(refs[1 + n_arrays + n_idle :])
    token = refs.pop(0)
    puts = len(adds) + sum(len(product[2]) for product in products)
    out = refs.pop(0) if puts else None
    parts = [None if product[2] else refs.pop(0) for product in products]
    token[...] = jnp.zeros_like(token)
    started = []

    def put(t, job, value):
        s_v, sems = refs
        at = len(started)
        i, j = at // table.shape[0], at % table.shape[0]
        slot = table[t, job]
        copy = pltpu.make_async_copy(s_v.at[i, j], out.at[t, jnp.maximum(slot, 0)], sems.at[i, j])
        s_v[i, j] = value
        started.append((slot >= 0, copy))

        @pl.when(slot >= 0)
        def _():
            copy.start()

    for job, ours, j, theirs, k in adds:
        for t in range(table.shape[0]):
            put(t, job, arrays[ours][t, j] + arrays[theirs][t, k])

    step = 2 * BLK
    for (train, pieces, sums, before), part in zip(products, parts):
        skip = 0
        if before is not None:
            skip = arrays[before].shape[1]
            part[:, :skip] = arrays[before][...]
        train = arrays[train]
        for m in range(train.shape[0] // step):
            for h in range(0, len(pieces), 2):
                q = jnp.concatenate([arrays[i][...] for i in pieces[h : h + 2]], axis=0)
                s = lax.dot_general(train[m * step : (m + 1) * step], q, NT, preferred_element_type=F32)
                for u in range(step // BLK):
                    for j in range(2):
                        t = m * (step // BLK) + u
                        value = s[u * BLK : (u + 1) * BLK, j * BLK : (j + 1) * BLK]
                        if sums:
                            job, at, column = sums[h + j]
                            put(t, job, value + arrays[at][t, column])
                        else:
                            part[t, skip + h + j] = value

    for named, copy in started:

        @pl.when(named)
        def _(copy=copy):
            copy.wait()


def stage(table, adds, products, out, slots, cost=0, wait=()):
    vmem = pl.BlockSpec(memory_space=pltpu.VMEM)
    arrays = []

    def index(array):
        for i, other in enumerate(arrays):
            if other is array:
                return i
        arrays.append(array)
        return len(arrays) - 1

    blocks = table.shape[0]
    adds = tuple((job, index(a), i, index(b), j) for job, (a, i), (b, j) in adds)
    shapes, out_specs, scratch = [jax.ShapeDtypeStruct((8, 128), F32)], [vmem], []
    puts = len(adds) + sum(len(product[2]) for product in products)
    if puts:
        shapes.append(jax.ShapeDtypeStruct((blocks, slots, BLK, BLK), F32))
        out_specs.append(pl.BlockSpec(memory_space=pl.ANY))
        scratch = [pltpu.VMEM((puts, blocks, BLK, BLK), F32), pltpu.SemaphoreType.DMA((puts, blocks))]
    spots = []
    for train, pieces, sums, before in products:
        if not sums:
            width = len(pieces) + (0 if before is None else before.shape[1])
            shapes.append(jax.ShapeDtypeStruct((blocks, width, BLK, BLK), F32))
            out_specs.append(vmem)
        spots.append((
            index(train), tuple(index(piece) for piece in pieces),
            tuple((job, index(array), i) for job, (array, i) in sums), None if before is None else index(before),
        ))
    args = [table, *arrays]
    specs = [pl.BlockSpec(memory_space=pltpu.SMEM)] + [vmem] * len(arrays)
    args += wait
    specs += [pl.BlockSpec(memory_space=pl.ANY)] * len(wait)
    aliased = bool(puts) and out is not None
    if aliased:
        args.append(out)
        specs.append(pl.BlockSpec(memory_space=pl.ANY))
    body = functools.partial(stage_kernel, adds, tuple(spots), len(arrays), len(wait) + aliased)
    token, *rest = pl.pallas_call(
        body,
        out_shape=shapes,
        in_specs=specs,
        out_specs=out_specs,
        scratch_shapes=scratch,
        input_output_aliases={len(args) - 1: 1} if aliased else {},
        compiler_params=pltpu.CompilerParams(vmem_limit_bytes=20 << 20),
        cost_estimate=pl.CostEstimate(flops=int(cost * 1.15e9), bytes_accessed=1, transcendentals=0),
        name="stage",
    )(*args)
    if puts:
        out = rest.pop(0)
    return token, out, rest


def pass_kernel(x_ref, y_ref):
    y_ref[...] = x_ref[...]


def stand(token, cost):
    return pl.pallas_call(
        pass_kernel,
        out_shape=jax.ShapeDtypeStruct(token.shape, token.dtype),
        compiler_params=pltpu.CompilerParams(vmem_limit_bytes=1 << 20),
        cost_estimate=pl.CostEstimate(flops=int(cost * 1.15e9), bytes_accessed=1, transcendentals=0),
        name="stand",
    )(token)


def after(x, *deps):
    return lax.optimization_barrier((x, *deps))[0]


def local_rings(train_grads, query_grads, pair_query, layer_slot, in_factor, out_factor):
    count = lax.axis_size("rows")
    height = count // 4

    def index(z, y, c):
        return (z % height * 2 + y) * 2 + c

    def ring(move):
        return [(i, index(*move(i // 4, i // 2 % 2, i % 2))) for i in range(count)]

    down = ring(lambda z, y, c: (z - 1, y, c))
    up = ring(lambda z, y, c: (z + 1, y, c))
    across = ring(lambda z, y, c: (z, 1 - y, c))
    twin = ring(lambda z, y, c: (z, y, 1 - c))

    def send(x, perm, name):
        with jax.named_scope("send_" + name):
            return lax.ppermute(x, "rows", perm)

    job = {}
    for letter, dz, dy in (("h", 0, 0), ("y", 0, 1), ("a", 1, 0), ("ya", 1, 1), ("f", 2, 0), ("yf", 2, 1), ("b", 3, 0), ("yb", 3, 1)):
        for dc in (0, 1):
            job[letter + str(dc)] = (dz * 2 + dy) * 2 + dc
    job["xa1"] = job.pop("ya1")
    other_name = {n: ("xa1" if n == "ya0" else "ya0" if n == "xa1" else n[:-1] + "10"[int(n[-1])]) for n in job}
    plan = [
        (("a0", "h0", down), ("y0", "h0", across)),
        (("b0", "h0", up), ("y1", "h1", across)),
        (("b1", "h1", up), ("ya0", "a0", across)),
        (("f0", "a0", down), ("yb0", "b0", across)),
        (("f1", "b1", up), ("yb1", "b1", across)),
        (("a1", "h1", down), ("yf0", "f0", across)),
        (("xa1", "y1", down), ("yf1", "f1", across)),
    ]
    work = {3: ["h0", "h1", "a0", "y0"], 4: ["b0", "y1", "b1", "ya0"], 5: ["f0", "yb0"], 6: ["f1", "yb1"], 7: ["a1", "yf0"]}
    exchange = (4, 6, 7)
    cost = {3: 1, 4: 1, 5: 1, 6: 1, 7: 1, 8: 12, 9: 1}
    stand_cost = 60
    slots = pair_query.shape[1]
    half = query_grads.shape[1] // 2
    core = lax.axis_index("rows") % 2
    low_half, high_half = query_grads[:, :half], query_grads[:, half:]
    raw = {"h0": jnp.where(core == 0, low_half, high_half)}
    raw["h1"] = send(jnp.where(core == 0, high_half, low_half), twin, "h1")
    raw["h1"], train_later = lax.optimization_barrier((raw["h1"], train_grads))
    for step in plan[:2]:
        for name, source, perm in step:
            raw[name] = send(raw[source], perm, name)
    high, low, own0, own1, table = prepare(
        layer_slot, pair_query, in_factor, out_factor, raw["h0"], raw["h1"], 2 * 8
    )
    got = {"h0": own0, "h1": own1}
    keep, rest, their_train, halves_token = make_halves(train_grads, send(train_later, twin, "train"))
    ours, theirs, open_jobs = {}, {}, list(other_name)
    out, tokens = None, []

    def ready_adds():
        done = [n for n in open_jobs if n in ours and other_name[n] in theirs]
        for n in done:
            open_jobs.remove(n)
        return [(job[n], ours[n], theirs[other_name[n]]) for n in done]

    held, columns, last_send = None, [], None
    for s in range(2, len(plan) + 1):
        names = [name for name, _, _ in plan[s - 2]]
        if s < 4:
            got[names[0]], got[names[1]] = make_ready(raw[names[0]], raw[names[1]], high, low)
        past = [got[name] for name in names] + (tokens if s > 3 else [halves_token] * (s == 3))
        if s < len(plan):
            for name, source, perm in plan[s]:
                if name == "xa1":
                    last_send = (name, source, perm, past)
                    continue
                deps = [v for v in past if v is not got[source]]
                got[name] = send(after(got[source], *deps), perm, name)
        if s not in work:
            continue
        pieces = [got[n] for n in work[s]]
        products = [(keep, pieces, (), None), (their_train, pieces, (), held)]
        token, _, (mine, held) = stage(table, [], products, None, slots, cost[s], tokens)
        tokens = [token]
        if s == len(plan) - 1:
            name, source, perm, past = last_send
            got[name] = send(after(got[source], *past, token), perm, name)
        ours.update({n: (mine, i) for i, n in enumerate(work[s])})
        columns += work[s]
        if s in exchange:
            part = send(held, twin, "part" + str(s))
            theirs.update({n: (part, i) for i, n in enumerate(columns)})
            held, columns = None, []
    late = {n: theirs.pop(n) for n in work[len(plan)]}
    adds = ready_adds()
    token, out, _ = stage(table, adds, [], None, slots, 1, [stand(tokens[0], stand_cost)])
    theirs.update(late)
    names = [name for name, _, _ in plan[-1]]
    pieces = [got[name] for name in names]
    twins = [send(after(piece, token), twin, "c" + name) for piece, name in zip(pieces, names)]
    _, _, (mine,) = stage(table, [], [(keep, pieces, (), None)], None, slots, cost[8], [token])
    ours.update({n: (mine, i) for i, n in enumerate(names)})
    adds = ready_adds()
    sums = tuple((job[other_name[name]], ours[other_name[name]]) for name in names)
    _, out, _ = stage(table, adds, [(rest, twins, sums, None)], out, slots, cost[9])
    return out


def local(train_grads, query_grads, pair_query, layer_slot, in_factor, out_factor):
    dims_count = lax.axis_size("dims")
    dims_index = lax.axis_index("dims")
    width = query_grads.shape[1]
    local_layers = width // SLOT
    slots = dims_index * local_layers + jnp.arange(local_layers, dtype=jnp.int32)
    onehot = (slots[:, None] == layer_slot[None, :]).astype(F32)
    a_fac = jnp.einsum("sl,lij->sij", onehot, in_factor, precision=lax.Precision.HIGHEST)
    b_fac = jnp.einsum("sl,lij->sij", onehot, out_factor, precision=lax.Precision.HIGHEST)
    nrow = query_grads.shape[0]
    query = query_grads.astype(F32).reshape(nrow, local_layers, PROJ, PROJ)
    left = jnp.einsum("sia,rsab->rsib", a_fac, query, precision=lax.Precision.HIGHEST)
    both = jnp.einsum("rsib,sbo->rsio", left, b_fac, precision=lax.Precision.HIGHEST)
    precond = both.reshape(nrow, width).astype(BF16)
    gathered = lax.all_gather(precond, "rows", axis=0, tiled=True)
    qblocks = gathered.reshape(gathered.shape[0] // BLK, BLK, width)
    tblocks = train_grads.reshape(train_grads.shape[0] // BLK, BLK, width)

    def one_block(items):
        tblock, ids = items
        chosen = qblocks[ids]
        return jnp.einsum("rg,kqg->krq", tblock, chosen, preferred_element_type=F32)

    partial_scores = lax.map(one_block, (tblocks, pair_query))
    summed = lax.psum(partial_scores, "dims")
    share = BLK // dims_count
    return lax.dynamic_slice_in_dim(summed, dims_index * share, share, 2)


def solution(mesh):
    in_specs = (
        P(("shard", "rows"), "dims"),
        P(("shard", "rows"), "dims"),
        P(("shard", "rows"), None),
        P(),
        P(),
        P(),
    )
    out_specs = P(("shard", "rows"), None, "dims", None)
    four = mesh.shape["rows"] == 16 and mesh.shape["dims"] == 1
    body = local_rings if four else local
    return jax.shard_map(body, mesh=mesh, in_specs=in_specs, out_specs=out_specs, check_vma=False)
```

```python
import functools

import jax
import jax.numpy as jnp
from jax import lax
from jax.experimental import pallas as pl
from jax.experimental.pallas import tpu as pltpu
from jax.sharding import PartitionSpec as P

PROJ = 16
BLK = 128
SLOT = PROJ * PROJ
F32 = jnp.float32
HALVES_LIMIT = 44
BF16 = jnp.bfloat16
NT = (((1,), (1,)), ((), ()))
BEHIND = pl.CostEstimate(flops=92 * 10**9, bytes_accessed=1, transcendentals=0)
SMALL = pl.CostEstimate(flops=10**9, bytes_accessed=1, transcendentals=0)


def split3(x):
    one = x.astype(BF16)
    rest = x - one.astype(F32)
    two = rest.astype(BF16)
    three = (rest - two.astype(F32)).astype(BF16)
    return jnp.concatenate([one, two, three], axis=1)


def split3(x):
    one = x.astype(BF16)
    rest = x - one.astype(F32)
    two = rest.astype(BF16)
    three = (rest - two.astype(F32)).astype(BF16)
    return one, two, three


def halves_kernel(train, twin_train, keep, rest, theirs, token, sems):
    token[...] = jnp.zeros_like(token)
    half = keep.shape[1]
    core = lax.axis_index("rows") & 1
    mine = pl.ds(pl.multiple_of(core * half, half), half)
    other = pl.ds(pl.multiple_of((1 - core) * half, half), half)
    copies = [
        pltpu.make_async_copy(train.at[:, mine], keep, sems.at[0]),
        pltpu.make_async_copy(twin_train.at[:, mine], theirs, sems.at[1]),
        pltpu.make_async_copy(train.at[:, other], rest, sems.at[2]),
    ]
    for copy in copies:
        copy.start()
    for copy in copies:
        copy.wait()


def make_halves(train, twin_train):
    side = jax.ShapeDtypeStruct((train.shape[0], train.shape[1] // 2), BF16)
    return pl.pallas_call(
        halves_kernel,
        out_shape=[side] * 3 + [jax.ShapeDtypeStruct((8, 128), F32)],
        in_specs=[pl.BlockSpec(memory_space=pl.ANY)] * 2,
        out_specs=[pl.BlockSpec(memory_space=pltpu.VMEM)] * 4,
        scratch_shapes=[pltpu.SemaphoreType.DMA((3,))],
        compiler_params=pltpu.CompilerParams(vmem_limit_bytes=HALVES_LIMIT << 20),
        cost_estimate=SMALL,
        name="halves",
    )(train, twin_train)


def precondition(x_refs, y_refs, high, low, skip):
    rows = x_refs[0].shape[0]
    for s in range(x_refs[0].shape[1] // SLOT):
        cols = slice(s * SLOT, (s + 1) * SLOT)
        x = jnp.concatenate([ref[:, cols] for ref in x_refs], axis=0)
        y = jnp.dot(x, high[skip + s], preferred_element_type=F32)
        y += jnp.dot(x, low[skip + s], preferred_element_type=F32)
        for i, ref in enumerate(y_refs):
            ref[:, cols] = y[i * rows : (i + 1) * rows].astype(BF16)


def prepare_kernel(layers, slot_ref, pair_ref, a_ref, b_ref, x0, x1, high_ref, low_ref, y0, y1, table, xa, xb):
    me = lax.axis_index("rows")
    core = me & 1
    row = lax.broadcasted_iota(jnp.int32, (PROJ, SLOT), 0)
    col = lax.broadcasted_iota(jnp.int32, (PROJ, SLOT), 1)
    pick_i = jnp.where(col // PROJ == row, 1.0, 0.0).astype(BF16)
    pick_o = jnp.where(col % PROJ == row, 1.0, 0.0).astype(BF16)
    total = 0.0
    for part in split3(b_ref[...]):
        total += jnp.dot(part, pick_o, preferred_element_type=F32)
    xb[...] = total
    for layer in range(layers):
        at = slice(layer * PROJ, (layer + 1) * PROJ)
        total = 0.0
        for part in split3(a_ref[at]):
            total += lax.dot_general(part, pick_i, (((0,), (0,)), ((), ())), preferred_element_type=F32)
        xa[at] = total

    @pl.loop(0, layers)
    def _(layer):
        slot = slot_ref[layer] - core * (layers // 2)

        @pl.when((slot >= 0) & (slot < layers // 2))
        def _():
            at = pl.multiple_of(layer * PROJ, PROJ)
            left = xa[pl.ds(at, PROJ), :]
            right = xb[pl.ds(at, PROJ), :]
            full = (left[:, None, :] * right[None, :, :]).reshape(SLOT, SLOT)
            high = full.astype(BF16)
            high_ref[slot] = high
            low_ref[slot] = (full - high.astype(F32)).astype(BF16)

    precondition([x0, x1], [y0, y1], high_ref, low_ref)
    blocks, slots = pair_ref.shape
    for t in range(blocks):
        for j in range(table.shape[1]):
            table[t, j] = -1
    for t in range(blocks):
        for k in range(slots):
            q = pair_ref[t, k]
            table[t, (((q >> 2) - (me >> 2)) & 3) * 4 + ((q ^ me) & 3)] = k


def prepare(layer_slot, pair_query, in_factor, out_factor, x0, x1, jobs):
    layers = in_factor.shape[0]
    a_rows = in_factor.reshape(layers * PROJ, PROJ)
    b_rows = out_factor.reshape(layers * PROJ, PROJ)
    vmem = pl.BlockSpec(memory_space=pltpu.VMEM)
    smem = pl.BlockSpec(memory_space=pltpu.SMEM)
    factor = jax.ShapeDtypeStruct((layers // 2, SLOT, SLOT), BF16)
    piece = jax.ShapeDtypeStruct(x0.shape, BF16)
    return pl.pallas_call(
        functools.partial(prepare_kernel, layers),
        out_shape=[factor, factor, piece, piece, jax.ShapeDtypeStruct((pair_query.shape[0], jobs), jnp.int32)],
        in_specs=[smem] * 2 + [vmem] * 4,
        out_specs=[vmem] * 4 + [smem],
        scratch_shapes=[
            pltpu.VMEM((layers * PROJ, SLOT), F32),
            pltpu.VMEM((layers * PROJ, SLOT), F32),
        ],
        compiler_params=pltpu.CompilerParams(vmem_limit_bytes=16 << 20),
        cost_estimate=BEHIND,
        name="prepare",
    )(layer_slot, pair_query, a_rows, b_rows, x0, x1)


def halves_kernel(train, twin_train, keep, rest, theirs, token, sems):
    token[...] = jnp.zeros_like(token)
    half = keep.shape[1]
    core = lax.axis_index("rows") & 1
    mine = pl.ds(pl.multiple_of(core * half, half), half)
    other = pl.ds(pl.multiple_of((1 - core) * half, half), half)
    copies = [
        pltpu.make_async_copy(train.at[:, mine], keep, sems.at[0]),
        pltpu.make_async_copy(twin_train.at[:, mine], theirs, sems.at[1]),
        pltpu.make_async_copy(train.at[:, other], rest, sems.at[2]),
    ]
    for copy in copies:
        copy.start()
    for copy in copies:
        copy.wait()


def make_halves(train, twin_train):
    side = jax.ShapeDtypeStruct((train.shape[0], train.shape[1] // 2), BF16)
    return pl.pallas_call(
        halves_kernel,
        out_shape=[side] * 3 + [jax.ShapeDtypeStruct((8, 128), F32)],
        in_specs=[pl.BlockSpec(memory_space=pl.ANY)] * 2,
        out_specs=[pl.BlockSpec(memory_space=pltpu.VMEM)] * 4,
        scratch_shapes=[pltpu.SemaphoreType.DMA((3,))],
        compiler_params=pltpu.CompilerParams(vmem_limit_bytes=HALVES_LIMIT << 20),
        cost_estimate=SMALL,
        name="halves",
    )(train, twin_train)


def precondition(x_refs, y_refs, high, low):
    rows = x_refs[0].shape[0]
    for s in range(x_refs[0].shape[1] // SLOT):
        cols = slice(s * SLOT, (s + 1) * SLOT)
        x = jnp.concatenate([ref[:, cols] for ref in x_refs], axis=0)
        y = jnp.dot(x, high[s], preferred_element_type=F32)
        y += jnp.dot(x, low[s], preferred_element_type=F32)
        for i, ref in enumerate(y_refs):
            ref[:, cols] = y[i * rows : (i + 1) * rows].astype(BF16)


def ready_kernel(x0, x1, high, low, y0, y1):
    precondition([x0, x1], [y0, y1], high, low)


def make_ready(x0, x1, high, low):
    return pl.pallas_call(
        ready_kernel,
        out_shape=[jax.ShapeDtypeStruct(x0.shape, BF16)] * 2,
        compiler_params=pltpu.CompilerParams(vmem_limit_bytes=10 << 20),
        cost_estimate=SMALL,
        name="ready",
    )(x0, x1, high, low)


def stage_kernel(adds, products, n_arrays, n_idle, *refs):
    table, arrays, refs = refs[0], refs[1 : 1 + n_arrays], list(refs[1 + n_arrays + n_idle :])
    token = refs.pop(0)
    puts = len(adds) + sum(len(product[2]) for product in products)
    out = refs.pop(0) if puts else None
    parts = [None if product[2] else refs.pop(0) for product in products]
    token[...] = jnp.zeros_like(token)
    started = []

    def put(t, job, value):
        s_v, sems = refs
        at = len(started)
        i, j = at // table.shape[0], at % table.shape[0]
        slot = table[t, job]
        copy = pltpu.make_async_copy(s_v.at[i, j], out.at[t, jnp.maximum(slot, 0)], sems.at[i, j])
        s_v[i, j] = value
        started.append((slot >= 0, copy))

        @pl.when(slot >= 0)
        def _():
            copy.start()

    for job, ours, j, theirs, k in adds:
        for t in range(table.shape[0]):
            put(t, job, arrays[ours][t, j] + arrays[theirs][t, k])

    step = 2 * BLK
    for (train, pieces, sums, before), part in zip(products, parts):
        skip = 0
        if before is not None:
            skip = arrays[before].shape[1]
            part[:, :skip] = arrays[before][...]
        train = arrays[train]
        for m in range(train.shape[0] // step):
            for h in range(0, len(pieces), 2):
                q = jnp.concatenate([arrays[i][...] for i in pieces[h : h + 2]], axis=0)
                s = lax.dot_general(train[m * step : (m + 1) * step], q, NT, preferred_element_type=F32)
                for u in range(step // BLK):
                    for j in range(2):
                        t = m * (step // BLK) + u
                        value = s[u * BLK : (u + 1) * BLK, j * BLK : (j + 1) * BLK]
                        if sums:
                            job, at, column = sums[h + j]
                            put(t, job, value + arrays[at][t, column])
                        else:
                            part[t, skip + h + j] = value

    for named, copy in started:

        @pl.when(named)
        def _(copy=copy):
            copy.wait()


def stage(table, adds, products, out, slots, cost=0, wait=()):
    vmem = pl.BlockSpec(memory_space=pltpu.VMEM)
    arrays = []

    def index(array):
        for i, other in enumerate(arrays):
            if other is array:
                return i
        arrays.append(array)
        return len(arrays) - 1

    blocks = table.shape[0]
    adds = tuple((job, index(a), i, index(b), j) for job, (a, i), (b, j) in adds)
    shapes, out_specs, scratch = [jax.ShapeDtypeStruct((8, 128), F32)], [vmem], []
    puts = len(adds) + sum(len(product[2]) for product in products)
    if puts:
        shapes.append(jax.ShapeDtypeStruct((blocks, slots, BLK, BLK), F32))
        out_specs.append(pl.BlockSpec(memory_space=pl.ANY))
        scratch = [pltpu.VMEM((puts, blocks, BLK, BLK), F32), pltpu.SemaphoreType.DMA((puts, blocks))]
    spots = []
    for train, pieces, sums, before in products:
        if not sums:
            width = len(pieces) + (0 if before is None else before.shape[1])
            shapes.append(jax.ShapeDtypeStruct((blocks, width, BLK, BLK), F32))
            out_specs.append(vmem)
        spots.append((
            index(train), tuple(index(piece) for piece in pieces),
            tuple((job, index(array), i) for job, (array, i) in sums), None if before is None else index(before),
        ))
    args = [table, *arrays]
    specs = [pl.BlockSpec(memory_space=pltpu.SMEM)] + [vmem] * len(arrays)
    args += wait
    specs += [pl.BlockSpec(memory_space=pl.ANY)] * len(wait)
    aliased = bool(puts) and out is not None
    if aliased:
        args.append(out)
        specs.append(pl.BlockSpec(memory_space=pl.ANY))
    body = functools.partial(stage_kernel, adds, tuple(spots), len(arrays), len(wait) + aliased)
    token, *rest = pl.pallas_call(
        body,
        out_shape=shapes,
        in_specs=specs,
        out_specs=out_specs,
        scratch_shapes=scratch,
        input_output_aliases={len(args) - 1: 1} if aliased else {},
        compiler_params=pltpu.CompilerParams(vmem_limit_bytes=20 << 20),
        cost_estimate=pl.CostEstimate(flops=int(cost * 1.15e9), bytes_accessed=1, transcendentals=0),
        name="stage",
    )(*args)
    if puts:
        out = rest.pop(0)
    return token, out, rest


def pass_kernel(x_ref, y_ref):
    y_ref[...] = x_ref[...]


def stand(token, cost):
    return pl.pallas_call(
        pass_kernel,
        out_shape=jax.ShapeDtypeStruct(token.shape, token.dtype),
        compiler_params=pltpu.CompilerParams(vmem_limit_bytes=1 << 20),
        cost_estimate=pl.CostEstimate(flops=int(cost * 1.15e9), bytes_accessed=1, transcendentals=0),
        name="stand",
    )(token)


def after(x, *deps):
    return lax.optimization_barrier((x, *deps))[0]


def local_rings(train_grads, query_grads, pair_query, layer_slot, in_factor, out_factor):
    count = lax.axis_size("rows")
    height = count // 4

    def index(z, y, c):
        return (z % height * 2 + y) * 2 + c

    def ring(move):
        return [(i, index(*move(i // 4, i // 2 % 2, i % 2))) for i in range(count)]

    down = ring(lambda z, y, c: (z - 1, y, c))
    up = ring(lambda z, y, c: (z + 1, y, c))
    across = ring(lambda z, y, c: (z, 1 - y, c))
    twin = ring(lambda z, y, c: (z, y, 1 - c))

    def send(x, perm, name):
        with jax.named_scope("send_" + name):
            return lax.ppermute(x, "rows", perm)

    job = {}
    for letter, dz, dy in (("h", 0, 0), ("y", 0, 1), ("a", 1, 0), ("ya", 1, 1), ("f", 2, 0), ("yf", 2, 1), ("b", 3, 0), ("yb", 3, 1)):
        for dc in (0, 1):
            job[letter + str(dc)] = (dz * 2 + dy) * 2 + dc
    job["xa1"] = job.pop("ya1")
    other_name = {n: ("xa1" if n == "ya0" else "ya0" if n == "xa1" else n[:-1] + "10"[int(n[-1])]) for n in job}
    plan = [
        (("a0", "h0", down), ("y0", "h0", across)),
        (("b0", "h0", up), ("y1", "h1", across)),
        (("b1", "h1", up), ("ya0", "a0", across)),
        (("f0", "a0", down), ("yb0", "b0", across)),
        (("f1", "b1", up), ("yb1", "b1", across)),
        (("a1", "h1", down), ("yf0", "f0", across)),
        (("xa1", "y1", down), ("yf1", "f1", across)),
    ]
    work = {3: ["h0", "h1", "a0", "y0"], 4: ["b0", "y1", "b1", "ya0"], 5: ["f0", "yb0"], 6: ["f1", "yb1"], 7: ["a1", "yf0"]}
    exchange = (4, 6, 7)
    cost = {3: 1, 4: 1, 5: 1, 6: 1, 7: 1, 8: 12, 9: 1}
    stand_cost = 60
    slots = pair_query.shape[1]
    half = query_grads.shape[1] // 2
    core = lax.axis_index("rows") % 2
    low_half, high_half = query_grads[:, :half], query_grads[:, half:]
    raw = {"h0": jnp.where(core == 0, low_half, high_half)}
    raw["h1"] = send(jnp.where(core == 0, high_half, low_half), twin, "h1")
    raw["h1"], train_later = lax.optimization_barrier((raw["h1"], train_grads))
    for step in plan[:2]:
        for name, source, perm in step:
            raw[name] = send(raw[source], perm, name)
    high, low, own0, own1, table = prepare(
        layer_slot, pair_query, in_factor, out_factor, raw["h0"], raw["h1"], 2 * 8
    )
    got = {"h0": own0, "h1": own1}
    keep, rest, their_train, halves_token = make_halves(train_grads, send(train_later, twin, "train"))
    ours, theirs, open_jobs = {}, {}, list(other_name)
    out, tokens = None, []

    def ready_adds():
        done = [n for n in open_jobs if n in ours and other_name[n] in theirs]
        for n in done:
            open_jobs.remove(n)
        return [(job[n], ours[n], theirs[other_name[n]]) for n in done]

    held, columns, last_send = None, [], None
    for s in range(2, len(plan) + 1):
        names = [name for name, _, _ in plan[s - 2]]
        if s < 4:
            got[names[0]], got[names[1]] = make_ready(raw[names[0]], raw[names[1]], high, low)
        past = [got[name] for name in names] + (tokens if s > 3 else [halves_token] * (s == 3))
        if s < len(plan):
            for name, source, perm in plan[s]:
                if name == "xa1":
                    last_send = (name, source, perm, past)
                    continue
                deps = [v for v in past if v is not got[source]]
                got[name] = send(after(got[source], *deps), perm, name)
        if s not in work:
            continue
        pieces = [got[n] for n in work[s]]
        products = [(keep, pieces, (), None), (their_train, pieces, (), held)]
        token, _, (mine, held) = stage(table, [], products, None, slots, cost[s], tokens)
        tokens = [token]
        if s == len(plan) - 1:
            name, source, perm, past = last_send
            got[name] = send(after(got[source], *past, token), perm, name)
        ours.update({n: (mine, i) for i, n in enumerate(work[s])})
        columns += work[s]
        if s in exchange:
            part = send(held, twin, "part" + str(s))
            theirs.update({n: (part, i) for i, n in enumerate(columns)})
            held, columns = None, []
    late = {n: theirs.pop(n) for n in work[len(plan)]}
    adds = ready_adds()
    token, out, _ = stage(table, adds, [], None, slots, 1, [stand(tokens[0], stand_cost)])
    theirs.update(late)
    names = [name for name, _, _ in plan[-1]]
    pieces = [got[name] for name in names]
    twins = [send(after(piece, token), twin, "c" + name) for piece, name in zip(pieces, names)]
    _, _, (mine,) = stage(table, [], [(keep, pieces, (), None)], None, slots, cost[8], [token])
    ours.update({n: (mine, i) for i, n in enumerate(names)})
    adds = ready_adds()
    sums = tuple((job[other_name[name]], ours[other_name[name]]) for name in names)
    _, out, _ = stage(table, adds, [(rest, twins, sums, None)], out, slots, cost[9])
    return out


def local(train_grads, query_grads, pair_query, layer_slot, in_factor, out_factor):
    dims_count = lax.axis_size("dims")
    dims_index = lax.axis_index("dims")
    width = query_grads.shape[1]
    local_layers = width // SLOT
    slots = dims_index * local_layers + jnp.arange(local_layers, dtype=jnp.int32)
    onehot = (slots[:, None] == layer_slot[None, :]).astype(F32)
    a_fac = jnp.einsum("sl,lij->sij", onehot, in_factor, precision=lax.Precision.HIGHEST)
    b_fac = jnp.einsum("sl,lij->sij", onehot, out_factor, precision=lax.Precision.HIGHEST)
    nrow = query_grads.shape[0]
    query = query_grads.astype(F32).reshape(nrow, local_layers, PROJ, PROJ)
    left = jnp.einsum("sia,rsab->rsib", a_fac, query, precision=lax.Precision.HIGHEST)
    both = jnp.einsum("rsib,sbo->rsio", left, b_fac, precision=lax.Precision.HIGHEST)
    precond = both.reshape(nrow, width).astype(BF16)
    gathered = lax.all_gather(precond, "rows", axis=0, tiled=True)
    qblocks = gathered.reshape(gathered.shape[0] // BLK, BLK, width)
    tblocks = train_grads.reshape(train_grads.shape[0] // BLK, BLK, width)

    def one_block(items):
        tblock, ids = items
        chosen = qblocks[ids]
        return jnp.einsum("rg,kqg->krq", tblock, chosen, preferred_element_type=F32)

    partial_scores = lax.map(one_block, (tblocks, pair_query))
    summed = lax.psum(partial_scores, "dims")
    share = BLK // dims_count
    return lax.dynamic_slice_in_dim(summed, dims_index * share, share, 2)


def solution(mesh):
    in_specs = (
        P(("shard", "rows"), "dims"),
        P(("shard", "rows"), "dims"),
        P(("shard", "rows"), None),
        P(),
        P(),
        P(),
    )
    out_specs = P(("shard", "rows"), None, "dims", None)
    four = mesh.shape["rows"] == 16 and mesh.shape["dims"] == 1
    body = local_rings if four else local
    return jax.shard_map(body, mesh=mesh, in_specs=in_specs, out_specs=out_specs, check_vma=False)
```

```python
import functools

import jax
import jax.numpy as jnp
from jax import lax
from jax.experimental import pallas as pl
from jax.experimental.pallas import tpu as pltpu
from jax.sharding import PartitionSpec as P

PROJ = 16
BLK = 128
SLOT = PROJ * PROJ
F32 = jnp.float32
HALVES_LIMIT = 44
BF16 = jnp.bfloat16
NT = (((1,), (1,)), ((), ()))
BEHIND = pl.CostEstimate(flops=92 * 10**9, bytes_accessed=1, transcendentals=0)
SMALL = pl.CostEstimate(flops=10**9, bytes_accessed=1, transcendentals=0)


def split3(x):
    one = x.astype(BF16)
    rest = x - one.astype(F32)
    two = rest.astype(BF16)
    three = (rest - two.astype(F32)).astype(BF16)
    return one, two, three


def prepare_kernel(layers, slot_ref, pair_ref, a_ref, b_ref, x0, x1, high_ref, low_ref, y0, y1, table, xa, xb):
    me = lax.axis_index("rows")
    core = me & 1
    row = lax.broadcasted_iota(jnp.int32, (PROJ, SLOT), 0)
    col = lax.broadcasted_iota(jnp.int32, (PROJ, SLOT), 1)
    pick_i = jnp.where(col // PROJ == row, 1.0, 0.0).astype(BF16)
    pick_o = jnp.where(col % PROJ == row, 1.0, 0.0).astype(BF16)
    total = 0.0
    for part in split3(b_ref[...]):
        total += jnp.dot(part, pick_o, preferred_element_type=F32)
    xb[...] = total
    for layer in range(layers):
        at = slice(layer * PROJ, (layer + 1) * PROJ)
        total = 0.0
        for part in split3(a_ref[at]):
            total += lax.dot_general(part, pick_i, (((0,), (0,)), ((), ())), preferred_element_type=F32)
        xa[at] = total

    @pl.loop(0, layers)
    def _(layer):
        slot = slot_ref[layer] - core * (layers // 2)

        @pl.when((slot >= 0) & (slot < layers // 2))
        def _():
            at = pl.multiple_of(layer * PROJ, PROJ)
            left = xa[pl.ds(at, PROJ), :]
            right = xb[pl.ds(at, PROJ), :]
            full = (left[:, None, :] * right[None, :, :]).reshape(SLOT, SLOT)
            high = full.astype(BF16)
            high_ref[slot] = high
            low_ref[slot] = (full - high.astype(F32)).astype(BF16)

    precondition([x0, x1], [y0, y1], high_ref, low_ref)
    blocks, slots = pair_ref.shape
    for t in range(blocks):
        for j in range(table.shape[1]):
            table[t, j] = -1
    for t in range(blocks):
        for k in range(slots):
            q = pair_ref[t, k]
            table[t, (((q >> 2) - (me >> 2)) & 3) * 4 + ((q ^ me) & 3)] = k


def prepare(layer_slot, pair_query, in_factor, out_factor, x0, x1, jobs):
    layers = in_factor.shape[0]
    a_rows = in_factor.reshape(layers * PROJ, PROJ)
    b_rows = out_factor.reshape(layers * PROJ, PROJ)
    vmem = pl.BlockSpec(memory_space=pltpu.VMEM)
    smem = pl.BlockSpec(memory_space=pltpu.SMEM)
    factor = jax.ShapeDtypeStruct((layers // 2, SLOT, SLOT), BF16)
    piece = jax.ShapeDtypeStruct(x0.shape, BF16)
    return pl.pallas_call(
        functools.partial(prepare_kernel, layers),
        out_shape=[factor, factor, piece, piece, jax.ShapeDtypeStruct((pair_query.shape[0], jobs), jnp.int32)],
        in_specs=[smem] * 2 + [vmem] * 4,
        out_specs=[vmem] * 4 + [smem],
        scratch_shapes=[
            pltpu.VMEM((layers * PROJ, SLOT), F32),
            pltpu.VMEM((layers * PROJ, SLOT), F32),
        ],
        compiler_params=pltpu.CompilerParams(vmem_limit_bytes=16 << 20),
        cost_estimate=BEHIND,
        name="prepare",
    )(layer_slot, pair_query, a_rows, b_rows, x0, x1)


def halves_kernel(train, twin_train, keep, rest, theirs, token, sems):
    token[...] = jnp.zeros_like(token)
    half = keep.shape[1]
    core = lax.axis_index("rows") & 1
    mine = pl.ds(pl.multiple_of(core * half, half), half)
    other = pl.ds(pl.multiple_of((1 - core) * half, half), half)
    copies = [
        pltpu.make_async_copy(train.at[:, mine], keep, sems.at[0]),
        pltpu.make_async_copy(twin_train.at[:, mine], theirs, sems.at[1]),
        pltpu.make_async_copy(train.at[:, other], rest, sems.at[2]),
    ]
    for copy in copies:
        copy.start()
    for copy in copies:
        copy.wait()


def make_halves(train, twin_train):
    side = jax.ShapeDtypeStruct((train.shape[0], train.shape[1] // 2), BF16)
    return pl.pallas_call(
        halves_kernel,
        out_shape=[side] * 3 + [jax.ShapeDtypeStruct((8, 128), F32)],
        in_specs=[pl.BlockSpec(memory_space=pl.ANY)] * 2,
        out_specs=[pl.BlockSpec(memory_space=pltpu.VMEM)] * 4,
        scratch_shapes=[pltpu.SemaphoreType.DMA((3,))],
        compiler_params=pltpu.CompilerParams(vmem_limit_bytes=HALVES_LIMIT << 20),
        cost_estimate=SMALL,
        name="halves",
    )(train, twin_train)


def precondition(x_refs, y_refs, high, low):
    rows = x_refs[0].shape[0]
    for s in range(x_refs[0].shape[1] // SLOT):
        cols = slice(s * SLOT, (s + 1) * SLOT)
        x = jnp.concatenate([ref[:, cols] for ref in x_refs], axis=0)
        y = jnp.dot(x, high[s], preferred_element_type=F32)
        y += jnp.dot(x, low[s], preferred_element_type=F32)
        for i, ref in enumerate(y_refs):
            ref[:, cols] = y[i * rows : (i + 1) * rows].astype(BF16)


def ready_kernel(x0, x1, high, low, y0, y1):
    precondition([x0, x1], [y0, y1], high, low)


def make_ready(x0, x1, high, low):
    return pl.pallas_call(
        ready_kernel,
        out_shape=[jax.ShapeDtypeStruct(x0.shape, BF16)] * 2,
        compiler_params=pltpu.CompilerParams(vmem_limit_bytes=10 << 20),
        cost_estimate=SMALL,
        name="ready",
    )(x0, x1, high, low)


def stage_kernel(adds, products, n_arrays, n_idle, *refs):
    table, arrays, refs = refs[0], refs[1 : 1 + n_arrays], list(refs[1 + n_arrays + n_idle :])
    token = refs.pop(0)
    puts = len(adds) + sum(len(product[2]) for product in products)
    out = refs.pop(0) if puts else None
    parts = [None if product[2] else refs.pop(0) for product in products]
    token[...] = jnp.zeros_like(token)
    started = []

    def put(t, job, value):
        s_v, sems = refs
        at = len(started)
        i, j = at // table.shape[0], at % table.shape[0]
        slot = table[t, job]
        copy = pltpu.make_async_copy(s_v.at[i, j], out.at[t, jnp.maximum(slot, 0)], sems.at[i, j])
        s_v[i, j] = value
        started.append((slot >= 0, copy))

        @pl.when(slot >= 0)
        def _():
            copy.start()

    for job, ours, j, theirs, k in adds:
        for t in range(table.shape[0]):
            put(t, job, arrays[ours][t, j] + arrays[theirs][t, k])

    step = 2 * BLK
    for (train, pieces, sums, before), part in zip(products, parts):
        skip = 0
        if before is not None:
            skip = arrays[before].shape[1]
            part[:, :skip] = arrays[before][...]
        train = arrays[train]
        for m in range(train.shape[0] // step):
            for h in range(0, len(pieces), 2):
                q = jnp.concatenate([arrays[i][...] for i in pieces[h : h + 2]], axis=0)
                s = lax.dot_general(train[m * step : (m + 1) * step], q, NT, preferred_element_type=F32)
                for u in range(step // BLK):
                    for j in range(2):
                        t = m * (step // BLK) + u
                        value = s[u * BLK : (u + 1) * BLK, j * BLK : (j + 1) * BLK]
                        if sums:
                            job, at, column = sums[h + j]
                            put(t, job, value + arrays[at][t, column])
                        else:
                            part[t, skip + h + j] = value

    for named, copy in started:

        @pl.when(named)
        def _(copy=copy):
            copy.wait()


def stage(table, adds, products, out, slots, cost=0, wait=()):
    vmem = pl.BlockSpec(memory_space=pltpu.VMEM)
    arrays = []

    def index(array):
        for i, other in enumerate(arrays):
            if other is array:
                return i
        arrays.append(array)
        return len(arrays) - 1

    blocks = table.shape[0]
    adds = tuple((job, index(a), i, index(b), j) for job, (a, i), (b, j) in adds)
    shapes, out_specs, scratch = [jax.ShapeDtypeStruct((8, 128), F32)], [vmem], []
    puts = len(adds) + sum(len(product[2]) for product in products)
    if puts:
        shapes.append(jax.ShapeDtypeStruct((blocks, slots, BLK, BLK), F32))
        out_specs.append(pl.BlockSpec(memory_space=pl.ANY))
        scratch = [pltpu.VMEM((puts, blocks, BLK, BLK), F32), pltpu.SemaphoreType.DMA((puts, blocks))]
    spots = []
    for train, pieces, sums, before in products:
        if not sums:
            width = len(pieces) + (0 if before is None else before.shape[1])
            shapes.append(jax.ShapeDtypeStruct((blocks, width, BLK, BLK), F32))
            out_specs.append(vmem)
        spots.append((
            index(train), tuple(index(piece) for piece in pieces),
            tuple((job, index(array), i) for job, (array, i) in sums), None if before is None else index(before),
        ))
    args = [table, *arrays]
    specs = [pl.BlockSpec(memory_space=pltpu.SMEM)] + [vmem] * len(arrays)
    args += wait
    specs += [pl.BlockSpec(memory_space=pl.ANY)] * len(wait)
    aliased = bool(puts) and out is not None
    if aliased:
        args.append(out)
        specs.append(pl.BlockSpec(memory_space=pl.ANY))
    body = functools.partial(stage_kernel, adds, tuple(spots), len(arrays), len(wait) + aliased)
    token, *rest = pl.pallas_call(
        body,
        out_shape=shapes,
        in_specs=specs,
        out_specs=out_specs,
        scratch_shapes=scratch,
        input_output_aliases={len(args) - 1: 1} if aliased else {},
        compiler_params=pltpu.CompilerParams(vmem_limit_bytes=20 << 20),
        cost_estimate=pl.CostEstimate(flops=int(cost * 1.15e9), bytes_accessed=1, transcendentals=0),
        name="stage",
    )(*args)
    if puts:
        out = rest.pop(0)
    return token, out, rest


def pass_kernel(x_ref, y_ref):
    y_ref[...] = x_ref[...]


def stand(token, cost):
    return pl.pallas_call(
        pass_kernel,
        out_shape=jax.ShapeDtypeStruct(token.shape, token.dtype),
        compiler_params=pltpu.CompilerParams(vmem_limit_bytes=1 << 20),
        cost_estimate=pl.CostEstimate(flops=int(cost * 1.15e9), bytes_accessed=1, transcendentals=0),
        name="stand",
    )(token)


def after(x, *deps):
    return lax.optimization_barrier((x, *deps))[0]


def local_rings(train_grads, query_grads, pair_query, layer_slot, in_factor, out_factor):
    count = lax.axis_size("rows")
    height = count // 4

    def index(z, y, c):
        return (z % height * 2 + y) * 2 + c

    def ring(move):
        return [(i, index(*move(i // 4, i // 2 % 2, i % 2))) for i in range(count)]

    down = ring(lambda z, y, c: (z - 1, y, c))
    up = ring(lambda z, y, c: (z + 1, y, c))
    across = ring(lambda z, y, c: (z, 1 - y, c))
    twin = ring(lambda z, y, c: (z, y, 1 - c))

    def send(x, perm, name):
        with jax.named_scope("send_" + name):
            return lax.ppermute(x, "rows", perm)

    job = {}
    for letter, dz, dy in (("h", 0, 0), ("y", 0, 1), ("a", 1, 0), ("ya", 1, 1), ("f", 2, 0), ("yf", 2, 1), ("b", 3, 0), ("yb", 3, 1)):
        for dc in (0, 1):
            job[letter + str(dc)] = (dz * 2 + dy) * 2 + dc
    job["xa1"] = job.pop("ya1")
    other_name = {n: ("xa1" if n == "ya0" else "ya0" if n == "xa1" else n[:-1] + "10"[int(n[-1])]) for n in job}
    plan = [
        (("a0", "h0", down), ("y0", "h0", across)),
        (("b0", "h0", up), ("y1", "h1", across)),
        (("b1", "h1", up), ("ya0", "a0", across)),
        (("f0", "a0", down), ("yb0", "b0", across)),
        (("f1", "b1", up), ("yb1", "b1", across)),
        (("a1", "h1", down), ("yf0", "f0", across)),
        (("xa1", "y1", down), ("yf1", "f1", across)),
    ]
    work = {3: ["h0", "h1", "a0", "y0"], 4: ["b0", "y1", "b1", "ya0"], 5: ["f0", "yb0"], 6: ["f1", "yb1"], 7: ["a1", "yf0"]}
    exchange = (4, 6, 7)
    cost = {3: 1, 4: 1, 5: 1, 6: 1, 7: 1, 8: 12, 9: 1}
    stand_cost = 60
    slots = pair_query.shape[1]
    half = query_grads.shape[1] // 2
    core = lax.axis_index("rows") % 2
    low_half, high_half = query_grads[:, :half], query_grads[:, half:]
    raw = {"h0": jnp.where(core == 0, low_half, high_half)}
    raw["h1"] = send(jnp.where(core == 0, high_half, low_half), twin, "h1")
    raw["h1"], train_later = lax.optimization_barrier((raw["h1"], train_grads))
    for step in plan[:2]:
        for name, source, perm in step:
            raw[name] = send(raw[source], perm, name)
    high, low, own0, own1, table = prepare(
        layer_slot, pair_query, in_factor, out_factor, raw["h0"], raw["h1"], 2 * 8
    )
    got = {"h0": own0, "h1": own1}
    keep, rest, their_train, halves_token = make_halves(train_grads, send(train_later, twin, "train"))
    ours, theirs, open_jobs = {}, {}, list(other_name)
    out, tokens = None, []

    def ready_adds():
        done = [n for n in open_jobs if n in ours and other_name[n] in theirs]
        for n in done:
            open_jobs.remove(n)
        return [(job[n], ours[n], theirs[other_name[n]]) for n in done]

    held, columns, last_send = None, [], None
    for s in range(2, len(plan) + 1):
        names = [name for name, _, _ in plan[s - 2]]
        if s < 4:
            got[names[0]], got[names[1]] = make_ready(raw[names[0]], raw[names[1]], high, low)
        past = [got[name] for name in names] + (tokens if s > 3 else [halves_token] * (s == 3))
        if s < len(plan):
            for name, source, perm in plan[s]:
                if name == "xa1":
                    last_send = (name, source, perm, past)
                    continue
                deps = [v for v in past if v is not got[source]]
                got[name] = send(after(got[source], *deps), perm, name)
        if s not in work:
            continue
        pieces = [got[n] for n in work[s]]
        products = [(keep, pieces, (), None), (their_train, pieces, (), held)]
        token, _, (mine, held) = stage(table, [], products, None, slots, cost[s], tokens)
        tokens = [token]
        if s == len(plan) - 1:
            name, source, perm, past = last_send
            got[name] = send(after(got[source], *past, token), perm, name)
        ours.update({n: (mine, i) for i, n in enumerate(work[s])})
        columns += work[s]
        if s in exchange:
            part = send(held, twin, "part" + str(s))
            theirs.update({n: (part, i) for i, n in enumerate(columns)})
            held, columns = None, []
    late = {n: theirs.pop(n) for n in work[len(plan)]}
    adds = ready_adds()
    token, out, _ = stage(table, adds, [], None, slots, 1, [stand(tokens[0], stand_cost)])
    theirs.update(late)
    names = [name for name, _, _ in plan[-1]]
    pieces = [got[name] for name in names]
    twins = [send(after(piece, token), twin, "c" + name) for piece, name in zip(pieces, names)]
    _, _, (mine,) = stage(table, [], [(keep, pieces, (), None)], None, slots, cost[8], [token])
    ours.update({n: (mine, i) for i, n in enumerate(names)})
    adds = ready_adds()
    sums = tuple((job[other_name[name]], ours[other_name[name]]) for name in names)
    _, out, _ = stage(table, adds, [(rest, twins, sums, None)], out, slots, cost[9])
    return out


def local(train_grads, query_grads, pair_query, layer_slot, in_factor, out_factor):
    dims_count = lax.axis_size("dims")
    dims_index = lax.axis_index("dims")
    width = query_grads.shape[1]
    local_layers = width // SLOT
    slots = dims_index * local_layers + jnp.arange(local_layers, dtype=jnp.int32)
    onehot = (slots[:, None] == layer_slot[None, :]).astype(F32)
    a_fac = jnp.einsum("sl,lij->sij", onehot, in_factor, precision=lax.Precision.HIGHEST)
    b_fac = jnp.einsum("sl,lij->sij", onehot, out_factor, precision=lax.Precision.HIGHEST)
    nrow = query_grads.shape[0]
    query = query_grads.astype(F32).reshape(nrow, local_layers, PROJ, PROJ)
    left = jnp.einsum("sia,rsab->rsib", a_fac, query, precision=lax.Precision.HIGHEST)
    both = jnp.einsum("rsib,sbo->rsio", left, b_fac, precision=lax.Precision.HIGHEST)
    precond = both.reshape(nrow, width).astype(BF16)
    gathered = lax.all_gather(precond, "rows", axis=0, tiled=True)
    qblocks = gathered.reshape(gathered.shape[0] // BLK, BLK, width)
    tblocks = train_grads.reshape(train_grads.shape[0] // BLK, BLK, width)

    def one_block(items):
        tblock, ids = items
        chosen = qblocks[ids]
        return jnp.einsum("rg,kqg->krq", tblock, chosen, preferred_element_type=F32)

    partial_scores = lax.map(one_block, (tblocks, pair_query))
    summed = lax.psum(partial_scores, "dims")
    share = BLK // dims_count
    return lax.dynamic_slice_in_dim(summed, dims_index * share, share, 2)


def solution(mesh):
    in_specs = (
        P(("shard", "rows"), "dims"),
        P(("shard", "rows"), "dims"),
        P(("shard", "rows"), None),
        P(),
        P(),
        P(),
    )
    out_specs = P(("shard", "rows"), None, "dims", None)
    four = mesh.shape["rows"] == 16 and mesh.shape["dims"] == 1
    body = local_rings if four else local
    return jax.shard_map(body, mesh=mesh, in_specs=in_specs, out_specs=out_specs, check_vma=False)
```

```python
import functools

import jax
import jax.numpy as jnp
from jax import lax
from jax.experimental import pallas as pl
from jax.experimental.pallas import tpu as pltpu
from jax.sharding import PartitionSpec as P

PROJ = 16
BLK = 128
SLOT = PROJ * PROJ
F32 = jnp.float32
HALVES_LIMIT = 44
BF16 = jnp.bfloat16
NT = (((1,), (1,)), ((), ()))
BEHIND = pl.CostEstimate(flops=92 * 10**9, bytes_accessed=1, transcendentals=0)
SMALL = pl.CostEstimate(flops=10**9, bytes_accessed=1, transcendentals=0)


def split3(x):
    one = x.astype(BF16)
    rest = x - one.astype(F32)
    two = rest.astype(BF16)
    three = (rest - two.astype(F32)).astype(BF16)
    return one, two, three


def prepare_kernel(layers, slot_ref, pair_ref, a_ref, b_ref, x0, x1, high_ref, low_ref, y0, y1, table, xa, xb):
    me = lax.axis_index("rows")
    core = me & 1
    row = lax.broadcasted_iota(jnp.int32, (PROJ, SLOT), 0)
    col = lax.broadcasted_iota(jnp.int32, (PROJ, SLOT), 1)
    pick_i = jnp.where(col // PROJ == row, 1.0, 0.0).astype(BF16)
    pick_o = jnp.where(col % PROJ == row, 1.0, 0.0).astype(BF16)
    total = 0.0
    for part in split3(b_ref[...]):
        total += jnp.dot(part, pick_o, preferred_element_type=F32)
    xb[...] = total
    for layer in range(layers):
        at = slice(layer * PROJ, (layer + 1) * PROJ)
        total = 0.0
        for part in split3(a_ref[at]):
            total += lax.dot_general(part, pick_i, (((0,), (0,)), ((), ())), preferred_element_type=F32)
        xa[at] = total

    @pl.loop(0, layers)
    def _(layer):
        slot = slot_ref[layer] - core * (layers // 2)

        @pl.when((slot >= 0) & (slot < layers // 2))
        def _():
            at = pl.multiple_of(layer * PROJ, PROJ)
            left = xa[pl.ds(at, PROJ), :]
            right = xb[pl.ds(at, PROJ), :]
            full = (left[:, None, :] * right[None, :, :]).reshape(SLOT, SLOT)
            high = full.astype(BF16)
            high_ref[slot] = high
            low_ref[slot] = (full - high.astype(F32)).astype(BF16)

    precondition([x0, x1], [y0, y1], high_ref, low_ref)
    blocks, slots = pair_ref.shape
    for t in range(blocks):
        for j in range(table.shape[1]):
            table[t, j] = -1
    for t in range(blocks):
        for k in range(slots):
            q = pair_ref[t, k]
            table[t, (((q >> 2) - (me >> 2)) & 3) * 4 + ((q ^ me) & 3)] = k


def prepare(layer_slot, pair_query, in_factor, out_factor, x0, x1, jobs):
    layers = in_factor.shape[0]
    a_rows = in_factor.reshape(layers * PROJ, PROJ)
    b_rows = out_factor.reshape(layers * PROJ, PROJ)
    vmem = pl.BlockSpec(memory_space=pltpu.VMEM)
    smem = pl.BlockSpec(memory_space=pltpu.SMEM)
    factor = jax.ShapeDtypeStruct((layers // 2, SLOT, SLOT), BF16)
    piece = jax.ShapeDtypeStruct(x0.shape, BF16)
    return pl.pallas_call(
        functools.partial(prepare_kernel, layers),
        out_shape=[factor, factor, piece, piece, jax.ShapeDtypeStruct((pair_query.shape[0], jobs), jnp.int32)],
        in_specs=[smem] * 2 + [vmem] * 4,
        out_specs=[vmem] * 4 + [smem],
        scratch_shapes=[
            pltpu.VMEM((layers * PROJ, SLOT), F32),
            pltpu.VMEM((layers * PROJ, SLOT), F32),
        ],
        compiler_params=pltpu.CompilerParams(vmem_limit_bytes=16 << 20),
        cost_estimate=BEHIND,
        name="prepare",
    )(layer_slot, pair_query, a_rows, b_rows, x0, x1)


def halves_kernel(train, twin_train, keep, rest, theirs, token, sems):
    token[...] = jnp.zeros_like(token)
    half = keep.shape[1]
    core = lax.axis_index("rows") & 1
    mine = pl.ds(pl.multiple_of(core * half, half), half)
    other = pl.ds(pl.multiple_of((1 - core) * half, half), half)
    copies = [
        pltpu.make_async_copy(train.at[:, mine], keep, sems.at[0]),
        pltpu.make_async_copy(twin_train.at[:, mine], theirs, sems.at[1]),
        pltpu.make_async_copy(train.at[:, other], rest, sems.at[2]),
    ]
    for copy in copies:
        copy.start()
    for copy in copies:
        copy.wait()


def make_halves(train, twin_train):
    side = jax.ShapeDtypeStruct((train.shape[0], train.shape[1] // 2), BF16)
    return pl.pallas_call(
        halves_kernel,
        out_shape=[side] * 3 + [jax.ShapeDtypeStruct((8, 128), F32)],
        in_specs=[pl.BlockSpec(memory_space=pl.ANY)] * 2,
        out_specs=[pl.BlockSpec(memory_space=pltpu.VMEM)] * 4,
        scratch_shapes=[pltpu.SemaphoreType.DMA((3,))],
        compiler_params=pltpu.CompilerParams(vmem_limit_bytes=HALVES_LIMIT << 20),
        cost_estimate=SMALL,
        name="halves",
    )(train, twin_train)


def precondition(x_refs, y_refs, high, low):
    rows = x_refs[0].shape[0]
    for s in range(x_refs[0].shape[1] // SLOT):
        cols = slice(s * SLOT, (s + 1) * SLOT)
        x = jnp.concatenate([ref[:, cols] for ref in x_refs], axis=0)
        y = jnp.dot(x, high[s], preferred_element_type=F32)
        y += jnp.dot(x, low[s], preferred_element_type=F32)
        for i, ref in enumerate(y_refs):
            ref[:, cols] = y[i * rows : (i + 1) * rows].astype(BF16)


def ready_kernel(x0, x1, high, low, y0, y1):
    precondition([x0, x1], [y0, y1], high, low)


def make_ready(x0, x1, high, low):
    return pl.pallas_call(
        ready_kernel,
        out_shape=[jax.ShapeDtypeStruct(x0.shape, BF16)] * 2,
        compiler_params=pltpu.CompilerParams(vmem_limit_bytes=10 << 20),
        cost_estimate=SMALL,
        name="ready",
    )(x0, x1, high, low)


def stage_kernel(adds, products, n_arrays, n_idle, *refs):
    table, arrays, refs = refs[0], refs[1 : 1 + n_arrays], list(refs[1 + n_arrays + n_idle :])
    token = refs.pop(0)
    puts = len(adds) + sum(len(product[2]) for product in products)
    out = refs.pop(0) if puts else None
    parts = [None if product[2] else refs.pop(0) for product in products]
    token[...] = jnp.zeros_like(token)
    started = []

    def put(t, job, value):
        s_v, sems = refs
        at = len(started)
        i, j = at // table.shape[0], at % table.shape[0]
        slot = table[t, job]
        copy = pltpu.make_async_copy(s_v.at[i, j], out.at[t, jnp.maximum(slot, 0)], sems.at[i, j])
        s_v[i, j] = value
        started.append((slot >= 0, copy))

        @pl.when(slot >= 0)
        def _():
            copy.start()

    for job, ours, j, theirs, k in adds:
        for t in range(table.shape[0]):
            put(t, job, arrays[ours][t, j] + arrays[theirs][t, k])

    for (train, pieces, sums, before), part in zip(products, parts):
        skip = 0
        step = 8 * BLK if sums else 2 * BLK
        if before is not None:
            skip = arrays[before].shape[1]
            part[:, :skip] = arrays[before][...]
        train = arrays[train]
        for m in range(train.shape[0] // step):
            for h in range(0, len(pieces), 2):
                q = jnp.concatenate([arrays[i][...] for i in pieces[h : h + 2]], axis=0)
                s = lax.dot_general(train[m * step : (m + 1) * step], q, NT, preferred_element_type=F32)
                for u in range(step // BLK):
                    for j in range(2):
                        t = m * (step // BLK) + u
                        value = s[u * BLK : (u + 1) * BLK, j * BLK : (j + 1) * BLK]
                        if sums:
                            job, at, column = sums[h + j]
                            put(t, job, value + arrays[at][t, column])
                        else:
                            part[t, skip + h + j] = value

    for named, copy in started:

        @pl.when(named)
        def _(copy=copy):
            copy.wait()


def stage(table, adds, products, out, slots, cost=0, wait=()):
    vmem = pl.BlockSpec(memory_space=pltpu.VMEM)
    arrays = []

    def index(array):
        for i, other in enumerate(arrays):
            if other is array:
                return i
        arrays.append(array)
        return len(arrays) - 1

    blocks = table.shape[0]
    adds = tuple((job, index(a), i, index(b), j) for job, (a, i), (b, j) in adds)
    shapes, out_specs, scratch = [jax.ShapeDtypeStruct((8, 128), F32)], [vmem], []
    puts = len(adds) + sum(len(product[2]) for product in products)
    if puts:
        shapes.append(jax.ShapeDtypeStruct((blocks, slots, BLK, BLK), F32))
        out_specs.append(pl.BlockSpec(memory_space=pl.ANY))
        scratch = [pltpu.VMEM((puts, blocks, BLK, BLK), F32), pltpu.SemaphoreType.DMA((puts, blocks))]
    spots = []
    for train, pieces, sums, before in products:
        if not sums:
            width = len(pieces) + (0 if before is None else before.shape[1])
            shapes.append(jax.ShapeDtypeStruct((blocks, width, BLK, BLK), F32))
            out_specs.append(vmem)
        spots.append((
            index(train), tuple(index(piece) for piece in pieces),
            tuple((job, index(array), i) for job, (array, i) in sums), None if before is None else index(before),
        ))
    args = [table, *arrays]
    specs = [pl.BlockSpec(memory_space=pltpu.SMEM)] + [vmem] * len(arrays)
    args += wait
    specs += [pl.BlockSpec(memory_space=pl.ANY)] * len(wait)
    aliased = bool(puts) and out is not None
    if aliased:
        args.append(out)
        specs.append(pl.BlockSpec(memory_space=pl.ANY))
    body = functools.partial(stage_kernel, adds, tuple(spots), len(arrays), len(wait) + aliased)
    token, *rest = pl.pallas_call(
        body,
        out_shape=shapes,
        in_specs=specs,
        out_specs=out_specs,
        scratch_shapes=scratch,
        input_output_aliases={len(args) - 1: 1} if aliased else {},
        compiler_params=pltpu.CompilerParams(vmem_limit_bytes=20 << 20),
        cost_estimate=pl.CostEstimate(flops=int(cost * 1.15e9), bytes_accessed=1, transcendentals=0),
        name="stage",
    )(*args)
    if puts:
        out = rest.pop(0)
    return token, out, rest


def pass_kernel(x_ref, y_ref):
    y_ref[...] = x_ref[...]


def stand(token, cost):
    return pl.pallas_call(
        pass_kernel,
        out_shape=jax.ShapeDtypeStruct(token.shape, token.dtype),
        compiler_params=pltpu.CompilerParams(vmem_limit_bytes=1 << 20),
        cost_estimate=pl.CostEstimate(flops=int(cost * 1.15e9), bytes_accessed=1, transcendentals=0),
        name="stand",
    )(token)


def after(x, *deps):
    return lax.optimization_barrier((x, *deps))[0]


def local_rings(train_grads, query_grads, pair_query, layer_slot, in_factor, out_factor):
    count = lax.axis_size("rows")
    height = count // 4

    def index(z, y, c):
        return (z % height * 2 + y) * 2 + c

    def ring(move):
        return [(i, index(*move(i // 4, i // 2 % 2, i % 2))) for i in range(count)]

    down = ring(lambda z, y, c: (z - 1, y, c))
    up = ring(lambda z, y, c: (z + 1, y, c))
    across = ring(lambda z, y, c: (z, 1 - y, c))
    twin = ring(lambda z, y, c: (z, y, 1 - c))

    def send(x, perm, name):
        with jax.named_scope("send_" + name):
            return lax.ppermute(x, "rows", perm)

    job = {}
    for letter, dz, dy in (("h", 0, 0), ("y", 0, 1), ("a", 1, 0), ("ya", 1, 1), ("f", 2, 0), ("yf", 2, 1), ("b", 3, 0), ("yb", 3, 1)):
        for dc in (0, 1):
            job[letter + str(dc)] = (dz * 2 + dy) * 2 + dc
    job["xa1"] = job.pop("ya1")
    other_name = {n: ("xa1" if n == "ya0" else "ya0" if n == "xa1" else n[:-1] + "10"[int(n[-1])]) for n in job}
    plan = [
        (("a0", "h0", down), ("y0", "h0", across)),
        (("b0", "h0", up), ("y1", "h1", across)),
        (("b1", "h1", up), ("ya0", "a0", across)),
        (("f0", "a0", down), ("yb0", "b0", across)),
        (("f1", "b1", up), ("yb1", "b1", across)),
        (("a1", "h1", down), ("yf0", "f0", across)),
        (("xa1", "y1", down), ("yf1", "f1", across)),
    ]
    work = {3: ["h0", "h1", "a0", "y0"], 4: ["b0", "y1", "b1", "ya0"], 5: ["f0", "yb0"], 6: ["f1", "yb1"], 7: ["a1", "yf0"]}
    exchange = (4, 6, 7)
    cost = {3: 2, 4: 2, 5: 2, 6: 2, 7: 2, 8: 12, 9: 1}
    stand_cost = 60
    slots = pair_query.shape[1]
    half = query_grads.shape[1] // 2
    core = lax.axis_index("rows") % 2
    low_half, high_half = query_grads[:, :half], query_grads[:, half:]
    raw = {"h0": jnp.where(core == 0, low_half, high_half)}
    raw["h1"] = send(jnp.where(core == 0, high_half, low_half), twin, "h1")
    raw["h1"], train_later = lax.optimization_barrier((raw["h1"], train_grads))
    for step in plan[:2]:
        for name, source, perm in step:
            raw[name] = send(raw[source], perm, name)
    high, low, own0, own1, table = prepare(
        layer_slot, pair_query, in_factor, out_factor, raw["h0"], raw["h1"], 2 * 8
    )
    got = {"h0": own0, "h1": own1}
    keep, rest, their_train, halves_token = make_halves(train_grads, send(train_later, twin, "train"))
    ours, theirs, open_jobs = {}, {}, list(other_name)
    out, tokens = None, []

    def ready_adds():
        done = [n for n in open_jobs if n in ours and other_name[n] in theirs]
        for n in done:
            open_jobs.remove(n)
        return [(job[n], ours[n], theirs[other_name[n]]) for n in done]

    held, columns, last_send = None, [], None
    for s in range(2, len(plan) + 1):
        names = [name for name, _, _ in plan[s - 2]]
        if s < 4:
            got[names[0]], got[names[1]] = make_ready(raw[names[0]], raw[names[1]], high, low)
        past = [got[name] for name in names] + (tokens if s > 3 else [halves_token] * (s == 3))
        if s < len(plan):
            for name, source, perm in plan[s]:
                if name == "xa1":
                    last_send = (name, source, perm, past)
                    continue
                deps = [v for v in past if v is not got[source]]
                got[name] = send(after(got[source], *deps), perm, name)
        if s not in work:
            continue
        pieces = [got[n] for n in work[s]]
        products = [(keep, pieces, (), None), (their_train, pieces, (), held)]
        token, _, (mine, held) = stage(table, [], products, None, slots, cost[s], tokens)
        tokens = [token]
        if s == len(plan) - 1:
            name, source, perm, past = last_send
            got[name] = send(after(got[source], *past, token), perm, name)
        ours.update({n: (mine, i) for i, n in enumerate(work[s])})
        columns += work[s]
        if s in exchange:
            part = send(held, twin, "part" + str(s))
            theirs.update({n: (part, i) for i, n in enumerate(columns)})
            held, columns = None, []
    late = {n: theirs.pop(n) for n in work[len(plan)]}
    adds = ready_adds()
    token, out, _ = stage(table, adds, [], None, slots, 1, [stand(tokens[0], stand_cost)])
    theirs.update(late)
    names = [name for name, _, _ in plan[-1]]
    pieces = [got[name] for name in names]
    twins = [send(after(piece, token), twin, "c" + name) for piece, name in zip(pieces, names)]
    _, _, (mine,) = stage(table, [], [(keep, pieces, (), None)], None, slots, cost[8], [token])
    ours.update({n: (mine, i) for i, n in enumerate(names)})
    adds = ready_adds()
    sums = tuple((job[other_name[name]], ours[other_name[name]]) for name in names)
    _, out, _ = stage(table, adds, [(rest, twins, sums, None)], out, slots, cost[9])
    return out


def local(train_grads, query_grads, pair_query, layer_slot, in_factor, out_factor):
    dims_count = lax.axis_size("dims")
    dims_index = lax.axis_index("dims")
    width = query_grads.shape[1]
    local_layers = width // SLOT
    slots = dims_index * local_layers + jnp.arange(local_layers, dtype=jnp.int32)
    onehot = (slots[:, None] == layer_slot[None, :]).astype(F32)
    a_fac = jnp.einsum("sl,lij->sij", onehot, in_factor, precision=lax.Precision.HIGHEST)
    b_fac = jnp.einsum("sl,lij->sij", onehot, out_factor, precision=lax.Precision.HIGHEST)
    nrow = query_grads.shape[0]
    query = query_grads.astype(F32).reshape(nrow, local_layers, PROJ, PROJ)
    left = jnp.einsum("sia,rsab->rsib", a_fac, query, precision=lax.Precision.HIGHEST)
    both = jnp.einsum("rsib,sbo->rsio", left, b_fac, precision=lax.Precision.HIGHEST)
    precond = both.reshape(nrow, width).astype(BF16)
    gathered = lax.all_gather(precond, "rows", axis=0, tiled=True)
    qblocks = gathered.reshape(gathered.shape[0] // BLK, BLK, width)
    tblocks = train_grads.reshape(train_grads.shape[0] // BLK, BLK, width)

    def one_block(items):
        tblock, ids = items
        chosen = qblocks[ids]
        return jnp.einsum("rg,kqg->krq", tblock, chosen, preferred_element_type=F32)

    partial_scores = lax.map(one_block, (tblocks, pair_query))
    summed = lax.psum(partial_scores, "dims")
    share = BLK // dims_count
    return lax.dynamic_slice_in_dim(summed, dims_index * share, share, 2)


def solution(mesh):
    in_specs = (
        P(("shard", "rows"), "dims"),
        P(("shard", "rows"), "dims"),
        P(("shard", "rows"), None),
        P(),
        P(),
        P(),
    )
    out_specs = P(("shard", "rows"), None, "dims", None)
    four = mesh.shape["rows"] == 16 and mesh.shape["dims"] == 1
    body = local_rings if four else local
    return jax.shard_map(body, mesh=mesh, in_specs=in_specs, out_specs=out_specs, check_vma=False)
```
